1024 devices in a mesh: dp: 16 (over z_hi, y), outer: 8 (over x), inner: 8 (over z_lo, core).
Axes of the slice: x: 8, y: 8, z: 8 (z_hi: 2, z_lo: 4; z = z_hi * 4 + z_lo), core: 2. Of those that a mesh axis runs over, the one named last changes fastest.
Arguments:
- tokens: bfloat16 [16384, 2080], P(('outer', 'inner')), may hold values from -6 to 6
- cotangent: bfloat16 [16384, 2080], P(('outer', 'inner')), may hold values from -6 to 6
- expert_id: int32 [16384], P(('outer', 'inner')), may hold values from 0 to 63
- slot_id: int32 [16384], P(('outer', 'inner')), may hold values from -1 to 3, as said below
- router: float32 [2080, 64], replicated, may hold values from -0.25 to 0.25
- w_in: bfloat16 [64, 2080, 3072], P(('outer', 'inner'), None, 'dp'), may hold values from -0.125 to 0.125
- w_out: bfloat16 [64, 3072, 2080], P(('outer', 'inner'), 'dp'), may hold values from -0.109375 to 0.109375
Outputs:
- mixed: bfloat16 [16384, 2080], P(('outer', 'inner'), 'dp')
- d_tokens: bfloat16 [16384, 2080], P(('outer', 'inner'), 'dp')
- d_w_in: bfloat16 [64, 2080, 3072], P(('outer', 'inner'), None, 'dp')
- d_w_out: bfloat16 [64, 3072, 2080], P(('outer', 'inner'), 'dp')
- d_router: float32 [2080, 64], P('dp')
The draws below stay inside these ranges and needn't reach their ends.
Inputs may be any that keep to these rules, and one draw needn't show every extreme that they name: `slot_id`: within a group, the tokens of one expert get slots 0, 1, 2, 3 in token order and -1 beyond the fourth; some group fills all 4 slots of some expert.
All inputs are finite; a program needn't handle non-finite values.
Results may differ from the reference program's by a relative error of at most 0.024.
Values may be sent and summed in bfloat16 or wider, within the bound.
A program may use at most 32 MiB of HBM per device.

```python
import jax
import jax.numpy as jnp
from jax import lax

D = 2080
FF = 3072
CAP = 4
EXPERTS = 64
TOKENS = 16384
N_DP = 16


def route_table(key):
    group_size = EXPERTS * CAP
    groups = TOKENS // group_size
    favored = jax.random.randint(jax.random.fold_in(key, 11), (groups, 1), 0, EXPERTS)
    spread_pick = jax.random.randint(jax.random.fold_in(key, 12), (groups, group_size), 0, EXPERTS)
    coin_flip = jax.random.randint(jax.random.fold_in(key, 13), (groups, group_size), 0, 4)
    experts = jnp.where(coin_flip == 0, favored, spread_pick).astype(jnp.int32)
    one_hot = (experts[:, :, None] == jnp.arange(EXPERTS, dtype=jnp.int32)[None, None, :]).astype(jnp.int32)
    ranking = jnp.cumsum(one_hot, axis=1) - 1
    own_rank = jnp.sum(ranking * one_hot, axis=2)
    slots = jnp.where(own_rank < CAP, own_rank, -1).astype(jnp.int32)
    return (experts.reshape(TOKENS), slots.reshape(TOKENS))


def draw_expert_id(key, part):
    experts, slots = route_table(key)
    return experts


def draw_slot_id(key, part):
    experts, slots = route_table(key)
    return slots


def level_of(key, shape, shards, smallest, largest):
    def one(dim, blocks):
        draws = jax.random.uniform(jax.random.fold_in(jax.random.fold_in(key, 6), dim), (blocks,), jnp.float32, smallest / len(shards), largest / len(shards))
        return jnp.repeat(jnp.exp(draws), shape[dim] // blocks).reshape((-1,) + (1,) * (len(shape) - dim - 1))

    gain = one(*shards[0])
    for cut in shards[1:]:
        gain = gain * one(*cut)
    return gain


def gaussian(own_key, dims, scale, limit, shards=(), kind=jnp.bfloat16):
    array = scale * jax.random.normal(own_key, dims, jnp.float32)
    if shards:
        array = array * level_of(own_key, dims, shards, -0.22, 0.18)
    return jnp.clip(array, -limit, limit).astype(kind)


def setup_inputs(seed: int = 0) -> dict:
    key_list = jax.random.split(jax.random.key(seed), 8)
    tokens = gaussian(key_list[0], (TOKENS, D), 1.0, 6.0, ((0, 64),))
    cotangent = gaussian(key_list[1], (TOKENS, D), 1.0, 6.0, ((0, 64),))
    expert_id = draw_expert_id(jax.random.fold_in(key_list[7], 71), 0)
    slot_id = draw_slot_id(jax.random.fold_in(key_list[7], 71), 0)
    router = gaussian(key_list[4], (D, EXPERTS), (D // 4) ** -0.5, 0.25, (), jnp.float32)
    w_in = gaussian(key_list[5], (EXPERTS, D, FF), D ** -0.5, 0.125, ((0, 64), (2, 16)))
    w_out = gaussian(key_list[6], (EXPERTS, FF, D), FF ** -0.5, 0.109375, ((0, 64), (1, 16)))
    return dict(tokens=tokens, cotangent=cotangent, expert_id=expert_id, slot_id=slot_id, router=router, w_in=w_in, w_out=w_out)


def gelu_tanh(values):
    return jax.nn.gelu(values, approximate=True)

def rounded(values):
    return lax.optimization_barrier(values.astype(jnp.bfloat16)).astype(jnp.float32)

def expert_math(operands):
    rows_in, rows_grad, weight_in, weight_out = operands
    slice_width = weight_in.shape[1] // N_DP
    pre_act = jnp.dot(rows_in, weight_in, preferred_element_type=jnp.float32)
    activated, pullback = jax.vjp(gelu_tanh, pre_act)
    hidden = activated.astype(jnp.bfloat16)
    grad_hidden = lax.dot_general(rows_grad, weight_out, (((1,), (1,)), ((), ())), preferred_element_type=jnp.float32)
    grad_pre = pullback(grad_hidden)[0].astype(jnp.bfloat16)
    grad_w_out = lax.dot_general(hidden, rows_grad, (((0,), (0,)), ((), ())), preferred_element_type=jnp.float32).astype(jnp.bfloat16)
    grad_w_in = lax.dot_general(rows_in, grad_pre, (((0,), (0,)), ((), ())), preferred_element_type=jnp.float32).astype(jnp.bfloat16)
    out_total = jnp.zeros(rows_in.shape, jnp.float32)
    in_total = jnp.zeros(rows_in.shape, jnp.float32)
    for shard_index in range(N_DP):
        start = shard_index * slice_width
        stop = start + slice_width
        out_total = out_total + rounded(jnp.dot(hidden[:, start:stop], weight_out[start:stop], preferred_element_type=jnp.float32))
        in_total = in_total + rounded(lax.dot_general(grad_pre[:, start:stop], weight_in[:, start:stop], (((1,), (1,)), ((), ())), preferred_element_type=jnp.float32))
    return (out_total.astype(jnp.bfloat16), in_total.astype(jnp.bfloat16), grad_w_in, grad_w_out)

def reference(tokens, cotangent, expert_id, slot_id, router, w_in, w_out):
    group_size = EXPERTS * CAP
    groups = TOKENS // group_size
    logits = jnp.dot(tokens.astype(jnp.float32), router, precision=lax.Precision.HIGHEST)
    chosen = expert_id[:, None] == jnp.arange(EXPERTS, dtype=jnp.int32)[None, :]
    gate_value = jax.nn.sigmoid(lax.optimization_barrier(jnp.sum(jnp.where(chosen, logits, 0.0), axis=1)))
    scaled = (gate_value[:, None] * cotangent.astype(jnp.float32)).astype(jnp.bfloat16)
    is_kept = slot_id >= 0
    position = jnp.where(is_kept, expert_id * CAP + slot_id, group_size).astype(jnp.int32)
    group_index = (jnp.arange(TOKENS, dtype=jnp.int32) // group_size).astype(jnp.int32)

    def dispatch(values):
        table = jnp.zeros((groups, group_size + 1, D), jnp.bfloat16)
        table = table.at[group_index, position].set(values)
        table = table[:, :group_size].reshape(groups, EXPERTS, CAP, D)
        return jnp.transpose(table, (1, 0, 2, 3)).reshape(EXPERTS, groups * CAP, D)

    def combine(values):
        table = jnp.transpose(values.reshape(EXPERTS, groups, CAP, D), (1, 0, 2, 3)).reshape(groups, group_size, D)
        table = jnp.concatenate([table, jnp.zeros((groups, 1, D), values.dtype)], axis=1)
        return table[group_index, position].astype(jnp.float32)
    expert_out, expert_in, grad_w_in, grad_w_out = lax.map(expert_math, (dispatch(tokens), dispatch(scaled), w_in, w_out))
    token_out = combine(expert_out)
    token_in = combine(expert_in)
    mixed = (gate_value[:, None] * token_out).astype(jnp.bfloat16)
    gate_grad = lax.optimization_barrier(jnp.sum(cotangent.astype(jnp.float32) * token_out, axis=1))
    logit_grad = gate_grad * gate_value * (1.0 - gate_value)
    weighted = jnp.where(chosen, logit_grad[:, None], 0.0)
    d_router = lax.dot_general(tokens.astype(jnp.float32), weighted, (((0,), (0,)), ((), ())), precision=lax.Precision.HIGHEST)
    router_part = logit_grad[:, None] * jnp.take(router.T, expert_id, axis=0)
    d_tokens = (token_in + router_part).astype(jnp.bfloat16)
    return (mixed, d_tokens, grad_w_in, grad_w_out, d_router)
```

```python
import functools

import jax
import jax.numpy as jnp
from jax import lax
from jax.experimental import pallas as pl
from jax.experimental.pallas import tpu as pltpu
from jax.sharding import PartitionSpec as P

BF = jnp.bfloat16
F32 = jnp.float32
NZ = 2
CAP = 4
VMEM_LIMIT = 56 * 1024 * 1024


def mm(a, b, ca=1, cb=0):
    return lax.dot_general(a, b, (((ca,), (cb,)), ((), ())), preferred_element_type=F32)


def split3(value):
    hi = value.astype(BF)
    rest = value - hi.astype(F32)
    mid = rest.astype(BF)
    low = (rest - mid.astype(F32)).astype(BF)
    return hi, mid, low


def stack3(value):
    hi, mid, low = (part.astype(F32) for part in split3(value[0:1]))
    row = lax.broadcasted_iota(jnp.int32, (16, value.shape[1]), 0)
    out = jnp.where(row == 0, hi, jnp.where(row == 1, mid, jnp.where(row == 2, low, 0.0)))
    return out.astype(BF)


def sum3(value):
    return value[0:1] + (value[1:2] + value[2:3])


def iota(shape, dim):
    return lax.broadcasted_iota(jnp.int32, shape, dim)


def log2(value):
    return value.bit_length() - 1


def kernel(
    nz,
    eid, sid, tokens, cot, router, w_in, w_out,
    mixed, d_tok, d_win, d_wout, d_router,
    s1a, s1b, r1a, r1b, s2a, s2t, s2b, main, tail, scl,
    wi2, wo2, wot, wip, wop, wtail, rvec, rpart, place_t, place_f,
    hid, gpr, rs_s, rs_r, rt_s, rt_r, tails_t, xs, fin,
    sbuf, drn, dr1, dro, drt, s3, r3, s4, r4,
    p1_ss, p1_rs, p2_ss, p2_rs, ag_ss, ag_rs, s_ss, s_rs, rm_ss, rm_rs, rt_ss, rt_rs,
    p3_ss, p3_rs, p4_ss, p4_rs, d1_ss, d1_rs, d2_ss, d2_rs,
):
    ndp, nx, ni = lax.axis_size("dp"), lax.axis_size("outer"), lax.axis_size("inner")
    ny = ndp // nz
    me_d, me_x, me_i = lax.axis_index("dp"), lax.axis_index("outer"), lax.axis_index("inner")
    me_y, me_z = lax.rem(me_d, ny), lax.div(me_d, ny)
    steps = ny // 2
    tcount, width = tokens.shape
    experts = nx * ni
    rows = experts * CAP
    ri, rx = nx * CAP, ni * CAP
    cb = nz * 128
    mainw = ndp * 128
    tw = width - mainw
    per = width // ndp
    ff = hid.shape[1]
    right, left = lax.rem(me_y + 1, ny), lax.rem(me_y + ny - 1, ny)
    half = rows // 2

    def send(src, dst, ss, rs, where):
        return pltpu.make_async_remote_copy(
            src_ref=src, dst_ref=dst, send_sem=ss, recv_sem=rs,
            device_id=where, device_id_type=pl.DeviceIdType.MESH,
        )

    def each(count, body, first=1):
        def step(k, carry):
            body(k)
            return carry

        lax.fori_loop(first, count, step, 0)

    def inner_at(k):
        return lax.rem(me_i + k, ni)

    def outer_at(k):
        return lax.rem(me_x + k, nx)

    def dp_at(k):
        return lax.rem(me_d + k, ndp)

    def y_at(k):
        return lax.rem(me_y + ny + k, ny)

    def far_dp(dz):
        return lax.rem(me_z + dz, nz) * ny + me_y

    def block(c, j):
        return main[c, j].reshape(rows, cb)

    def lanes_of(j):
        return pl.ds(pl.multiple_of(j * cb, 128), cb)

    barrier = pltpu.get_barrier_semaphore()

    def hello(where):
        pl.semaphore_signal(barrier, inc=1, device_id=where, device_id_type=pl.DeviceIdType.MESH)

    each(ni, lambda k: hello({"inner": inner_at(k)}))
    each(nx, lambda k: hello({"outer": outer_at(k)}))
    each(ndp, lambda k: hello({"dp": dp_at(k)}))
    for dz in range(1, nz):
        each(ni, lambda k, dz=dz: hello({"dp": far_dp(dz), "inner": inner_at(k)}))

    e, s = eid[...], sid[...]
    spot = jnp.where(s >= 0, (e & (ni - 1)) * ri + (e >> log2(ni)) * CAP + s, -1)
    place = (iota((rows, tcount), 0) == spot).astype(F32)
    place_t[...] = place.astype(BF)
    own = lanes_of(me_y)
    s1a[:, :, :cb] = mm(place_t[...], tokens[:, own]).astype(BF).reshape(ni, ri, cb)
    spread_a = (iota((tw, 128), 0) == iota((tw, 128), 1)).astype(BF)
    spread_b = (iota((tw, 128), 0) + tw == iota((tw, 128), 1)).astype(BF)
    ends = mm(tokens[:, mainw:width], spread_a) + mm(cot[:, mainw:width], spread_b)
    s1a[:, :, cb:] = mm(place_t[...], ends.astype(BF)).astype(BF).reshape(ni, ri, 128)
    r1a[me_i] = s1a[me_i]
    pl.semaphore_wait(barrier, (ni - 1) * nz + (nx - 1) + (ndp - 1))

    def p1(c, s1, r1, peer, slot):
        return send(s1.at[peer], r1.at[slot], p1_ss.at[c, peer], p1_rs.at[c, slot], {"inner": peer})

    def p1_start(c, s1, r1):
        each(ni, lambda k: p1(c, s1, r1, inner_at(k), me_i).start())

    def p1_wait(c, s1, r1):
        each(ni, lambda k: p1(c, s1, r1, inner_at(k), inner_at(k)).wait())

    p1_start(0, s1a, r1a)
    s1b[...] = mm(place_t[...], cot[:, own]).astype(BF).reshape(ni, ri, cb)
    r1b[me_i] = s1b[me_i]
    p1_start(1, s1b, r1b)

    place_f[...] = place.T.astype(BF)
    row, col = iota((rows, rows), 0), iota((rows, rows), 1)
    same_slot = (row & (CAP - 1)) == (col & (CAP - 1))
    row4, col4 = row >> log2(CAP), col >> log2(CAP)
    swap = (
        same_slot
        & ((row4 >> log2(ni)) == (col4 & (nx - 1)))
        & ((row4 & (ni - 1)) == (col4 >> log2(nx)))
    ).astype(BF)
    onehot = (iota((8, experts), 1) == me_x * ni + me_i).astype(F32)
    rvec[:, :width] = lax.dot_general(
        onehot, router[...], (((1,), (1,)), ((), ())),
        precision=lax.Precision.HIGHEST, preferred_element_type=F32,
    )
    rvec[:, width:] = jnp.zeros((8, rvec.shape[1] - width), F32)

    def p2(q, src, dst_of, peer, slot):
        return send(src.at[peer], dst_of(slot), p2_ss.at[q, peer], p2_rs.at[q, slot], {"outer": peer})

    def p2_start(q, src, dst_of):
        each(nx, lambda k: p2(q, src, dst_of, outer_at(k), me_x).start())

    def p2_wait(q, src, dst_of):
        each(nx, lambda k: p2(q, src, dst_of, outer_at(k), outer_at(k)).wait())

    def to_a(x):
        return main.at[0, me_y, x]

    def to_b(x):
        return main.at[1, me_y, x]

    def to_t(x):
        return tail.at[x]

    p1_wait(0, s1a, r1a)
    s2a[...] = mm(swap, r1a[:, :, :cb].reshape(rows, cb)).astype(BF).reshape(nx, rx, cb)
    p2_start(0, s2a, to_a)
    s2t[...] = mm(swap, r1a[:, :, cb:].reshape(rows, 128)).astype(BF).reshape(nx, rx, 128)
    p2_start(1, s2t, to_t)
    main[0, me_y, me_x] = s2a[me_x]
    tail[me_x] = s2t[me_x]
    p1_wait(1, s1b, r1b)
    s2b[...] = mm(swap, r1b[...].reshape(rows, cb)).astype(BF).reshape(nx, rx, cb)
    p2_start(2, s2b, to_b)
    main[1, me_y, me_x] = s2b[me_x]

    wi2[:width] = w_in[0]
    wi2[width:] = jnp.zeros((wi2.shape[0] - width, ff), BF)
    wo2[:, :width] = w_out[0]
    wo2[:, width:] = jnp.zeros((ff, wo2.shape[1] - width), BF)

    def ag(c, way, t, j):
        ref = main.at[c, j]
        if t == steps - 1:
            ref = main.at[c, j, pl.ds(0 if way == 0 else nx // 2, nx // 2)]
        peer = right if way == 0 else left
        return send(ref, ref, ag_ss.at[c, way, t], ag_rs.at[c, way, t], {"dp": me_z * ny + peer})

    def ag_mine(c, way, t):
        return ag(c, way, t, y_at(-t if way == 0 else t))

    def ag_theirs(c, way, t):
        return ag(c, way, t, y_at(-t - 1 if way == 0 else t + 1))

    p2_wait(0, s2a, to_a)
    for way in range(2):
        ag_mine(0, way, 0).start()
    p2_wait(2, s2b, to_b)
    for way in range(2):
        ag_mine(1, way, 0).start()
    p2_wait(1, s2t, to_t)

    def reorder(d, carry):
        y, z = lax.rem(d, ny), lax.div(d, ny)
        at = pl.ds(pl.multiple_of(d * 128, 128), 256)
        part = pl.ds(pl.multiple_of(z * 128, 128), 128)
        pick = (iota((256, 128), 0) == iota((256, 128), 1) + 2 * d).astype(BF)
        wop[y, :, part] = mm(wo2[:, at], pick).astype(BF)
        pick = (iota((128, 256), 1) == iota((128, 256), 0) + 2 * d).astype(BF)
        wip[y, part, :] = mm(pick, wi2[at, :]).astype(BF)
        return carry

    def tail_weights():
        shape = (ny * 16, wo2.shape[1])
        q, y = iota(shape, 0) & 15, iota(shape, 0) >> 4
        for first, ref, dim in ((0, wo2, 1), (2 * nz, wi2, 0)):
            qq = q - first
            want = ((qq >> 1) * ny + y) * per + 128 + (qq & 1)
            pick = ((want == iota(shape, 1)) & (qq >= 0) & (qq < 2 * nz)).astype(BF)
            wtail[0 if first == 0 else 1] = mm(pick, ref[...], 1, dim).astype(BF)

    rpart[...] = stack3(rvec[...])
    tail_rows = tail[...].reshape(rows, 128)
    pre = mm(tail_rows, wi2[mainw:, :])
    lg3 = mm(rpart[:, mainw:], tail_rows, 1, 1)

    def forward_block(j, pre, lg3):
        at = lanes_of(j)
        return (
            pre + mm(block(0, j), wi2[at, :]),
            lg3 + mm(rpart[:, at], block(0, j), 1, 1),
        )

    pre, lg3 = forward_block(me_y, pre, lg3)
    wot[...] = mm(
        wo2[:, mainw:],
        ((iota((128, 128), 0) + tw == iota((128, 128), 1)) & (iota((128, 128), 0) < tw)).astype(BF),
    ).astype(BF)
    for t in range(1, steps + 1):
        for c in range(2):
            for way in range(2):
                ag_theirs(c, way, t - 1).wait_recv()
                if t < steps:
                    ag_mine(c, way, t).start()
            if c == 0:
                pre, lg3 = forward_block(y_at(t), pre, lg3)
                if t < steps:
                    pre, lg3 = forward_block(y_at(-t), pre, lg3)
                    many = -(-ndp // (steps - 1))
                    lax.fori_loop((t - 1) * many, min(ndp, t * many), reorder, 0)
        if t == 1:
            tail_weights()

    gate_row = jax.nn.sigmoid(sum3(lg3))
    xs[...] = jnp.zeros(xs.shape, F32)
    xs[0:1, :] = gate_row
    gate_col = xs[...].T[:, 0:1]
    root, cubic = 0.7978845608028654, 0.044715
    tanh = jnp.tanh(root * (pre + cubic * (pre * pre * pre)))
    hid[...] = (0.5 * pre * (1.0 + tanh)).astype(BF)
    slope = 0.5 * (1.0 + tanh) + 0.5 * pre * (1.0 - tanh * tanh) * (
        root * (1.0 + (3.0 * cubic) * (pre * pre))
    )
    tails_scaled = (gate_col * tail_rows.astype(F32)).astype(BF)
    grad = mm(tails_scaled, wot[...], 1, 1)

    def scale_block(j, total):
        scaled = (gate_col * block(1, j).astype(F32)).astype(BF)
        scl[j] = scaled
        return total + mm(scaled, wo2[:, lanes_of(j)], 1, 1)

    grad = lax.fori_loop(0, ny, scale_block, grad)
    gpr[...] = (slope * grad).astype(BF)

    def rs_copy(way, t, c):
        src, dst = rs_s.at[way, t, c], rs_r.at[way, t, c]
        if t == 0:
            part = pl.ds(0 if way == 0 else half, half)
            src, dst = rs_s.at[0, 0, c, part], rs_r.at[way, 0, c, part]
        peer = right if way == 0 else left
        return send(src, dst, rm_ss.at[way, t, c], rm_rs.at[way, t, c], {"dp": me_z * ny + peer})

    def rt_copy(way, t):
        peer = right if way == 0 else left
        return send(rt_s.at[way, t], rt_r.at[way, t], rt_ss.at[way, t], rt_rs.at[way, t], {"dp": me_z * ny + peer})

    def partial(c, b):
        if c == 0:
            return mm(hid[...], wop[b])
        return mm(gpr[...], wip[b], 1, 1)

    for c in range(2):
        rs_s[0, 0, c] = partial(c, y_at(steps)).astype(BF)
        for way in range(2):
            rs_copy(way, 0, c).start()
    tails_t[...] = (mm(wtail[0], hid[...], 1, 1) + mm(wtail[1], gpr[...], 1, 1)).reshape(ny, 16, rows)
    rt_s[0, 0] = tails_t[y_at(steps)].astype(BF)
    rt_copy(0, 0).start()

    product = hid[...].astype(F32) * grad
    dots = lax.dot_general(
        jnp.ones((8, ff), F32), product, (((1,), (1,)), ((), ())),
        precision=lax.Precision.HIGHEST, preferred_element_type=F32,
    )
    sbuf[me_d] = dots[0:1]

    def s_copy(k, slot):
        return send(sbuf.at[me_d], sbuf.at[slot], s_ss.at[dp_at(k)], s_rs.at[slot], {"dp": dp_at(k)})

    each(ndp, lambda k: s_copy(k, me_d).start())

    def win_block(j, carry):
        at = lanes_of(j)
        d_win[0, at, :] = mm(block(0, j), gpr[...], 0, 0).astype(BF)
        d_wout[0, :, at] = mm(hid[...], scl[j], 0, 0).astype(BF)
        return carry

    def d1_copy(k, slot):
        return send(dr1.at[me_i], dr1.at[slot], d1_ss.at[inner_at(k)], d1_rs.at[slot], {"inner": inner_at(k)})

    def d2_copy(k, slot):
        return send(dro.at[me_x], dro.at[slot], d2_ss.at[outer_at(k)], d2_rs.at[slot], {"outer": outer_at(k)})

    for t in range(1, steps):
        for c in range(2):
            for way in range(2):
                b = y_at(steps - t if way == 0 else t - steps)
                value = partial(c, b)
                rs_copy(way, t - 1, c).wait_recv()
                if t == 1:
                    part = slice(0, half) if way == 0 else slice(half, rows)
                    rest = slice(half, rows) if way == 0 else slice(0, half)
                    rs_s[way, t, c, part] = (value[part] + rs_r[way, 0, c, part].astype(F32)).astype(BF)
                    rs_s[way, t, c, rest] = value[rest].astype(BF)
                else:
                    rs_s[way, t, c] = (value + rs_r[way, t - 1, c].astype(F32)).astype(BF)
                rs_copy(way, t, c).start()
        for way in range(2):
            ends = tails_t[y_at(steps - t if way == 0 else t - steps)]
            if way == 0 or t > 1:
                rt_copy(way, t - 1).wait_recv()
                ends = ends + rt_r[way, t - 1].astype(F32)
            rt_s[way, t] = ends.astype(BF)
            rt_copy(way, t).start()
        if t == 1:
            each(ndp, lambda k: s_copy(k, dp_at(k)).wait())
            total = sbuf[0]
            for k in range(1, ndp):
                total = total + sbuf[k]
            lg_row = total * (1.0 - gate_row)
            xs[1:2, :] = lg_row
            lgs = stack3(lg_row)
            for j in range(ny):
                drn[:, j * cb:(j + 1) * cb] = jnp.broadcast_to(sum3(mm(lgs, block(0, j))), (8, cb))
            drn[:, mainw:] = jnp.broadcast_to(sum3(mm(lgs, tail_rows)), (8, 128))
            piece = drn[:, pl.ds(pl.multiple_of(me_d * 128, 128), 256)]
            dr1[me_i] = pltpu.roll(piece, lax.rem(256 - 2 * me_d, 256), 1)[0:1]
            each(ni, lambda k: d1_copy(k, me_i).start())
        if t == 2 or steps == 2:
            each(ni, lambda k: d1_copy(k, inner_at(k)).wait())
            for k in range(ni):
                dro[me_x, k:k + 1] = dr1[k]
            each(nx, lambda k: d2_copy(k, me_x).start())
        many = -(-ny // (steps - 1))
        lax.fori_loop((t - 1) * many, min(ny, t * many), win_block, 0)
    d_win[0, mainw:width, :] = mm(tail_rows, gpr[...], 0, 0)[:tw].astype(BF)
    d_wout[0, :, mainw:width] = mm(hid[...], tails_scaled, 0, 0)[:, tw:2 * tw].astype(BF)

    rc = []
    for z in range(nz):
        d = z * ny + me_y
        piece = rvec[:, pl.ds(pl.multiple_of(d * 128, 128), 256)]
        mine = (me_z == z).astype(F32)
        rc.append(pltpu.roll(piece, lax.rem(256 - 2 * d, 256), 1)[0:1] * mine)
    lg_row = xs[1:2, :]
    for c in range(2):
        fin[c] = partial(c, me_y)
    ends = tails_t[me_y]
    for way in range(2):
        rt_copy(way, steps - 1).wait_recv()
        ends = ends + rt_r[way, steps - 1].astype(F32)
    xs[8:24, :] = ends
    for q in range(2 * nz):
        xs[8 + q:9 + q, :] = xs[8 + q:9 + q, :] * gate_row
        z, k = q // 2, q % 2
        at = 8 + 2 * nz + q
        xs[at:at + 1, :] = xs[at:at + 1, :] + lg_row * rc[z][:, 128 + k:129 + k]
    turned = xs[...].T
    lg_col = turned[:, 1:2]
    s3[:, :, nz * 256:] = turned.astype(BF).reshape(nx, rx, 128)
    for c in range(2):
        for way in range(2):
            rs_copy(way, steps - 1, c).wait_recv()
        value = fin[c] + rs_r[0, steps - 1, c].astype(F32) + rs_r[1, steps - 1, c].astype(F32)
        for z in range(nz):
            piece = value[:, z * 128:(z + 1) * 128]
            piece = gate_col * piece if c == 0 else piece + lg_col * rc[z][:, :128]
            first = z * 256 + c * 128
            s3[:, :, first:first + 128] = piece.astype(BF).reshape(nx, rx, 128)

    def p3(peer, slot):
        return send(s3.at[peer], r3.at[slot], p3_ss.at[peer], p3_rs.at[slot], {"outer": peer})

    each(nx, lambda k: p3(outer_at(k), me_x).start())
    r3[me_x] = s3[me_x]
    swap_back = (
        same_slot
        & ((row4 >> log2(nx)) == (col4 & (ni - 1)))
        & ((row4 & (nx - 1)) == (col4 >> log2(ni)))
    ).astype(BF)
    each(nx, lambda k: p3(outer_at(k), outer_at(k)).wait())
    ends = mm(swap_back, r3[:, :, nz * 256:].reshape(rows, 128)).astype(BF).reshape(ni, ri, 128)
    for z in range(nz):
        value = mm(swap_back, r3[:, :, z * 256:(z + 1) * 256].reshape(rows, 256))
        s4[z, :, :, :256] = value.astype(BF).reshape(ni, ri, 256)
        s4[z, :, :, 256:] = ends

    def p4(z, peer, slot_z, slot_i):
        return send(
            s4.at[z, peer], r4.at[slot_z, slot_i], p4_ss.at[z, peer], p4_rs.at[slot_z, slot_i],
            {"dp": z * ny + me_y, "inner": peer},
        )

    def p4_all(act):
        for dz in range(nz):
            z = lax.rem(me_z + dz, nz)
            each(ni, lambda k, z=z: act(z, inner_at(k)), 1 if dz == 0 else 0)

    p4_all(lambda z, peer: p4(z, peer, me_z, me_i).start())
    r4[me_z, me_i] = s4[me_z, me_i]
    each(nx, lambda k: d2_copy(k, outer_at(k)).wait())
    drt[...] = jnp.zeros(drt.shape, F32)
    drt[:experts] = dro[...].reshape(experts, 256)
    d_router[...] = drt[...].T[:per, :experts]

    for c in range(2):
        for way in range(2):
            for t in range(steps):
                ag_mine(c, way, t).wait_send()
                rs_copy(way, t, c).wait_send()
    for way in range(2):
        for t in range(steps):
            if way == 0 or t > 0:
                rt_copy(way, t).wait_send()

    p4_all(lambda z, peer: p4(z, peer, z, peer).wait())
    value = r4[0].astype(F32)
    for z in range(1, nz):
        value = value + r4[z].astype(F32)
    value = value.astype(BF).reshape(rows, 384)
    result = mm(place_f[...], value)
    ends = pltpu.roll(result[:, 256:], lax.rem(128 - 8 - 2 * me_z, 128), 1)
    mixed[:, :128] = result[:, :128].astype(BF)
    mixed[:, 128:per] = ends[:, 0:2].astype(BF)
    d_tok[:, :128] = result[:, 128:256].astype(BF)
    d_tok[:, 128:per] = ends[:, 2 * nz:2 * nz + 2].astype(BF)


def on_device(nz, tokens, cotangent, expert_id, slot_id, router, w_in, w_out):
    ndp, nx, ni = lax.axis_size("dp"), lax.axis_size("outer"), lax.axis_size("inner")
    ny = ndp // nz
    steps = ny // 2
    tcount, width = tokens.shape
    experts = nx * ni
    rows = experts * CAP
    ri, rx = nx * CAP, ni * CAP
    cb = nz * 128
    padded = (ndp + 1) * 128
    per = width // ndp
    ff = w_in.shape[2]
    dma = pltpu.SemaphoreType.DMA
    vm = pltpu.VMEM
    scratch = [
        vm((ni, ri, cb + 128), BF), vm((ni, ri, cb), BF), vm((ni, ri, cb + 128), BF), vm((ni, ri, cb), BF),
        vm((nx, rx, cb), BF), vm((nx, rx, 128), BF), vm((nx, rx, cb), BF),
        vm((2, ny, nx, rx, cb), BF), vm((nx, rx, 128), BF), vm((ny, rows, cb), BF),
        vm((padded, ff), BF), vm((ff, padded), BF), vm((ff, 128), BF), vm((ny, cb, ff), BF), vm((ny, ff, cb), BF),
        vm((2, ny * 16, ff), BF), vm((8, padded), F32), vm((16, padded), BF), vm((rows, tcount), BF), vm((tcount, rows), BF),
        vm((rows, ff), BF), vm((rows, ff), BF), vm((2, steps, 2, rows, cb), BF), vm((2, steps, 2, rows, cb), BF),
        vm((2, steps, 16, rows), BF), vm((2, steps, 16, rows), BF), vm((ny, 16, rows), F32), vm((128, rows), F32), vm((2, rows, cb), F32),
        vm((ndp, 1, rows), F32), vm((8, padded), F32), vm((ni, 1, 256), F32), vm((nx, ni, 256), F32), vm((128, 256), F32),
        vm((nx, rx, nz * 256 + 128), BF), vm((nx, rx, nz * 256 + 128), BF), vm((nz, ni, ri, 384), BF), vm((nz, ni, ri, 384), BF),
        dma((2, ni)), dma((2, ni)), dma((3, nx)), dma((3, nx)), dma((2, 2, steps)), dma((2, 2, steps)), dma((ndp,)), dma((ndp,)),
        dma((2, steps, 2)), dma((2, steps, 2)), dma((2, steps)), dma((2, steps)),
        dma((nx,)), dma((nx,)), dma((nz, ni)), dma((nz, ni)), dma((ni,)), dma((ni,)), dma((nx,)), dma((nx,)),
    ]
    shape = jax.ShapeDtypeStruct
    return pl.pallas_call(
        functools.partial(kernel, nz),
        out_shape=(
            shape((tcount, per), BF), shape((tcount, per), BF),
            shape(w_in.shape, BF), shape(w_out.shape, BF), shape((per, experts), F32),
        ),
        in_specs=[pl.BlockSpec(memory_space=pltpu.VMEM)] * 7,
        out_specs=tuple([pl.BlockSpec(memory_space=pltpu.VMEM)] * 5),
        scratch_shapes=scratch,
        compiler_params=pltpu.CompilerParams(
            collective_id=0, has_side_effects=True, vmem_limit_bytes=VMEM_LIMIT
        ),
    )(expert_id.reshape(1, tcount), slot_id.reshape(1, tcount), tokens, cotangent, router, w_in, w_out)


def build(mesh, nz):
    return jax.shard_map(
        functools.partial(on_device, nz),
        mesh=mesh,
        in_specs=(
            P(("outer", "inner"), None),
            P(("outer", "inner"), None),
            P(("outer", "inner")),
            P(("outer", "inner")),
            P(),
            P(("outer", "inner"), None, "dp"),
            P(("outer", "inner"), "dp", None),
        ),
        out_specs=(
            P(("outer", "inner"), "dp"),
            P(("outer", "inner"), "dp"),
            P(("outer", "inner"), None, "dp"),
            P(("outer", "inner"), "dp", None),
            P("dp", None),
        ),
        check_vma=False,
    )


def solution(mesh):
    return build(mesh, NZ)
```

```python
import functools

import jax
import jax.numpy as jnp
from jax import lax
from jax.experimental import pallas as pl
from jax.experimental.pallas import tpu as pltpu
from jax.sharding import PartitionSpec as P

BF = jnp.bfloat16
F32 = jnp.float32
NZ = 2
CAP = 4
VMEM_LIMIT = 60 * 1024 * 1024


def mm(a, b, ca=1, cb=0):
    return lax.dot_general(a, b, (((ca,), (cb,)), ((), ())), preferred_element_type=F32)


def split3(value):
    hi = value.astype(BF)
    rest = value - hi.astype(F32)
    mid = rest.astype(BF)
    low = (rest - mid.astype(F32)).astype(BF)
    return hi, mid, low


def stack3(value):
    hi, mid, low = (part.astype(F32) for part in split3(value[0:1]))
    row = lax.broadcasted_iota(jnp.int32, (16, value.shape[1]), 0)
    out = jnp.where(row == 0, hi, jnp.where(row == 1, mid, jnp.where(row == 2, low, 0.0)))
    return out.astype(BF)


def sum3(value):
    return value[0:1] + (value[1:2] + value[2:3])


def iota(shape, dim):
    return lax.broadcasted_iota(jnp.int32, shape, dim)


def log2(value):
    return value.bit_length() - 1


def kernel(
    nz,
    eid, sid, tokens, cot, router, w_in, w_out,
    mixed, d_tok, d_win, d_wout, d_router,
    tokx, cotx, ends_t, rrow, wir, wor, dwi, dwo,
    s1a, s1b, r1a, r1b, s2a, s2t, s2b, r2b, main, tail, scl, swaps,
    wi2, wo2, wot, wip, wop, wtail, rvec, rpart, place_t,
    hid, gpr, rs_s, rs_r, rt_s, rt_r, tails_t, xs,
    sbuf, drn, dr1, dro, drt, s3m, r3m, s3t, r3t, s4m, r4m, s4t, r4t,
    loc, a1_ss, a1_rs, a2_ss, a2_rs, b1_ss, b1_rs, b2_ss, b2_rs,
    ag_ss, ag_rs, s_ss, s_rs, rm_ss, rm_rs, rt_ss, rt_rs,
    p3_ss, p3_rs, p4_ss, p4_rs, d1_ss, d1_rs, d2_ss, d2_rs,
):
    ndp, nx, ni = lax.axis_size("dp"), lax.axis_size("outer"), lax.axis_size("inner")
    ny = ndp // nz
    me_d, me_x, me_i = lax.axis_index("dp"), lax.axis_index("outer"), lax.axis_index("inner")
    me_y, me_z = lax.rem(me_d, ny), lax.div(me_d, ny)
    steps = ny // 2
    width, tcount = tokens.shape
    experts = nx * ni
    rows = experts * CAP
    ri, rx = nx * CAP, ni * CAP
    cb = nz * 128
    mainw = ndp * 128
    tw = width - mainw
    per = width // ndp
    ff = hid.shape[1]
    right, left = lax.rem(me_y + 1, ny), lax.rem(me_y + ny - 1, ny)
    half = rows // 2

    def send(src, dst, ss, rs, where):
        return pltpu.make_async_remote_copy(
            src_ref=src, dst_ref=dst, send_sem=ss, recv_sem=rs,
            device_id=where, device_id_type=pl.DeviceIdType.MESH,
        )

    def each(count, body, first=1):
        def step(k, carry):
            body(k)
            return carry

        lax.fori_loop(first, count, step, 0)

    def inner_at(k):
        return lax.rem(me_i + k, ni)

    def outer_at(k):
        return lax.rem(me_x + k, nx)

    def dp_at(k):
        return lax.rem(me_d + k, ndp)

    def y_at(k):
        return lax.rem(me_y + ny + k, ny)

    def far_dp(dz):
        return lax.rem(me_z + dz, nz) * ny + me_y

    def block(c, j):
        return main[c, j].reshape(rows, cb)

    def lanes_of(j):
        return pl.ds(pl.multiple_of(j * cb, 128), cb)

    barrier = pltpu.get_barrier_semaphore()

    def hello(where):
        pl.semaphore_signal(barrier, inc=1, device_id=where, device_id_type=pl.DeviceIdType.MESH)

    each(ni, lambda k: hello({"inner": inner_at(k)}))
    each(nx, lambda k: hello({"outer": outer_at(k)}))
    each(ndp, lambda k: hello({"dp": dp_at(k)}))
    for dz in range(1, nz):
        each(ni, lambda k, dz=dz: hello({"dp": far_dp(dz), "inner": inner_at(k)}))

    own = lanes_of(me_y)
    loads = [
        pltpu.make_async_copy(src, dst, loc.at[i])
        for i, (src, dst) in enumerate((
            (tokens.at[own], tokx),
            (tokens.at[pl.ds(mainw, tw)], ends_t.at[pl.ds(0, tw)]),
            (cot.at[pl.ds(mainw, tw)], ends_t.at[pl.ds(tw, tw)]),
            (cot.at[own], cotx),
            (router.at[pl.ds(pl.multiple_of(me_x * ni, ni), ni)], rrow),
            (w_in.at[0], wir),
            (w_out.at[0], wor),
        ))
    ]
    for load in loads:
        load.start()

    e, s = eid[...], sid[...]
    spot = jnp.where(s >= 0, (e & (ni - 1)) * ri + (e >> log2(ni)) * CAP + s, -1)
    place_t[...] = (iota((rows, tcount), 0) == spot).astype(BF)
    ends_t[2 * tw:] = jnp.zeros((128 - 2 * tw, tcount), BF)
    for load in loads[:3]:
        load.wait()
    s1a[:, :, :cb] = mm(place_t[...], tokx[...], 1, 1).astype(BF).reshape(ni, ri, cb)
    s1a[:, :, cb:] = mm(place_t[...], ends_t[...], 1, 1).astype(BF).reshape(ni, ri, 128)
    pl.semaphore_wait(barrier, (ni - 1) * nz + (nx - 1) + (ndp - 1))

    def a1(peer, slot):
        return send(s1a.at[peer], r1a.at[slot], a1_ss.at[peer], a1_rs.at[slot], {"inner": peer})

    def b1(peer, slot):
        return send(s1b.at[peer], r1b.at[slot], b1_ss.at[peer], b1_rs.at[slot], {"outer": peer})

    each(ni, lambda k: a1(inner_at(k), me_i).start())
    place_b = (iota((rows, tcount), 0) == jnp.where(s >= 0, e * CAP + s, -1)).astype(BF)
    loads[3].wait()
    s1b[...] = mm(place_b, cotx[...], 1, 1).astype(BF).reshape(nx, rx, cb)
    each(nx, lambda k: b1(outer_at(k), me_x).start())
    r1a[me_i] = s1a[me_i]
    r1b[me_x] = s1b[me_x]

    row, col = iota((rows, rows), 0), iota((rows, rows), 1)
    same_slot = (row & (CAP - 1)) == (col & (CAP - 1))
    row4, col4 = row >> log2(CAP), col >> log2(CAP)
    swaps[0] = (
        same_slot
        & ((row4 >> log2(ni)) == (col4 & (nx - 1)))
        & ((row4 & (ni - 1)) == (col4 >> log2(nx)))
    ).astype(BF)
    swaps[1] = (
        same_slot
        & ((row4 >> log2(nx)) == (col4 & (ni - 1)))
        & ((row4 & (nx - 1)) == (col4 >> log2(ni)))
    ).astype(BF)

    def a2(q, peer, slot):
        src = (s2a if q == 0 else s2t).at[peer]
        dst = main.at[0, me_y, slot] if q == 0 else tail.at[slot]
        return send(src, dst, a2_ss.at[q, peer], a2_rs.at[q, slot], {"outer": peer})

    def b2(peer, slot):
        return send(s2b.at[peer], r2b.at[slot], b2_ss.at[peer], b2_rs.at[slot], {"inner": peer})

    each(ni, lambda k: a1(inner_at(k), inner_at(k)).wait())
    s2a[...] = mm(swaps[0], r1a[:, :, :cb].reshape(rows, cb)).astype(BF).reshape(nx, rx, cb)
    each(nx, lambda k: a2(0, outer_at(k), me_x).start())
    s2t[...] = mm(swaps[0], r1a[:, :, cb:].reshape(rows, 128)).astype(BF).reshape(nx, rx, 128)
    each(nx, lambda k: a2(1, outer_at(k), me_x).start())
    each(nx, lambda k: b1(outer_at(k), outer_at(k)).wait())
    s2b[...] = mm(swaps[1], r1b[...].reshape(rows, cb)).astype(BF).reshape(ni, ri, cb)
    each(ni, lambda k: b2(inner_at(k), me_i).start())
    main[0, me_y, me_x] = s2a[me_x]
    tail[me_x] = s2t[me_x]
    r2b[me_i] = s2b[me_i]

    for load in loads[4:]:
        load.wait()
    rvec[:, :width] = jnp.broadcast_to(rrow[pl.ds(me_i, 1), :], (8, width))
    rvec[:, width:] = jnp.zeros((8, rvec.shape[1] - width), F32)
    wi2[:, :width] = wir[...]
    wi2[:, width:] = jnp.zeros((ff, wi2.shape[1] - width), BF)
    wo2[:, :width] = wor[...]
    wo2[:, width:] = jnp.zeros((ff, wo2.shape[1] - width), BF)

    def ag(c, way, t, j):
        ref = main.at[c, j]
        if t == steps - 1:
            ref = main.at[c, j, pl.ds(0 if way == 0 else nx // 2, nx // 2)]
        peer = right if way == 0 else left
        return send(ref, ref, ag_ss.at[c, way, t], ag_rs.at[c, way, t], {"dp": me_z * ny + peer})

    def ag_mine(c, way, t):
        return ag(c, way, t, y_at(-t if way == 0 else t))

    def ag_theirs(c, way, t):
        return ag(c, way, t, y_at(-t - 1 if way == 0 else t + 1))

    each(nx, lambda k: a2(0, outer_at(k), outer_at(k)).wait())
    for way in range(2):
        ag_mine(0, way, 0).start()
    each(ni, lambda k: b2(inner_at(k), inner_at(k)).wait())
    main[1, me_y] = mm(swaps[0], r2b[...].reshape(rows, cb)).astype(BF).reshape(nx, rx, cb)
    for way in range(2):
        ag_mine(1, way, 0).start()
    each(nx, lambda k: a2(1, outer_at(k), outer_at(k)).wait())

    def reorder(d, carry):
        y, z = lax.rem(d, ny), lax.div(d, ny)
        at = pl.ds(pl.multiple_of(d * 128, 128), 256)
        part = pl.ds(pl.multiple_of(z * 128, 128), 128)
        pick = (iota((256, 128), 0) == iota((256, 128), 1) + 2 * d).astype(BF)
        wop[y, :, part] = mm(wo2[:, at], pick).astype(BF)
        wip[y, :, part] = mm(wi2[:, at], pick).astype(BF)
        return carry

    def tail_weights():
        shape = (ny * 16, wo2.shape[1])
        q, y = iota(shape, 0) & 15, iota(shape, 0) >> 4
        for first, ref in ((0, wo2), (2 * nz, wi2)):
            qq = q - first
            want = ((qq >> 1) * ny + y) * per + 128 + (qq & 1)
            pick = ((want == iota(shape, 1)) & (qq >= 0) & (qq < 2 * nz)).astype(BF)
            wtail[0 if first == 0 else 1] = mm(pick, ref[...], 1, 1).astype(BF)

    rpart[...] = stack3(rvec[...])
    tail_rows = tail[...].reshape(rows, 128)
    pre = mm(tail_rows, wi2[:, mainw:], 1, 1)
    lg3 = mm(rpart[:, mainw:], tail_rows, 1, 1)

    def forward_block(j, pre, lg3):
        at = lanes_of(j)
        return (
            pre + mm(block(0, j), wi2[:, at], 1, 1),
            lg3 + mm(rpart[:, at], block(0, j), 1, 1),
        )

    pre, lg3 = forward_block(me_y, pre, lg3)
    wot[...] = mm(
        wo2[:, mainw:],
        ((iota((128, 128), 0) + tw == iota((128, 128), 1)) & (iota((128, 128), 0) < tw)).astype(BF),
    ).astype(BF)
    for t in range(1, steps + 1):
        for c in range(2):
            for way in range(2):
                ag_theirs(c, way, t - 1).wait_recv()
                if t < steps:
                    ag_mine(c, way, t).start()
            if c == 0:
                pre, lg3 = forward_block(y_at(t), pre, lg3)
                if t < steps:
                    pre, lg3 = forward_block(y_at(-t), pre, lg3)
                    many = -(-ndp // (steps - 1))
                    lax.fori_loop((t - 1) * many, min(ndp, t * many), reorder, 0)
        if t == 1:
            tail_weights()

    gate_row = jax.nn.sigmoid(sum3(lg3))
    xs[...] = jnp.zeros(xs.shape, F32)
    xs[0:1, :] = gate_row
    gate_col = xs[...].T[:, 0:1]
    root, cubic = 0.7978845608028654, 0.044715
    tanh = jnp.tanh(root * (pre + cubic * (pre * pre * pre)))
    hid[...] = (0.5 * pre * (1.0 + tanh)).astype(BF)

    def rs_copy(way, t, c, z):
        src, dst = rs_s.at[way, t, c, z], rs_r.at[way, t, c, z]
        if t == 0:
            part = pl.ds(0 if way == 0 else half, half)
            src, dst = rs_s.at[0, 0, c, z, part], rs_r.at[way, 0, c, z, part]
        peer = right if way == 0 else left
        return send(src, dst, rm_ss.at[way, t, c, z], rm_rs.at[way, t, c, z], {"dp": me_z * ny + peer})

    def rt_copy(way, t):
        peer = right if way == 0 else left
        return send(rt_s.at[way, t], rt_r.at[way, t], rt_ss.at[way, t], rt_rs.at[way, t], {"dp": me_z * ny + peer})

    def partial(c, b):
        return mm(hid[...], wop[b]) if c == 0 else mm(gpr[...], wip[b])

    def cut(value, z):
        return value[:, z * 128:(z + 1) * 128]

    def rs_step(c, t):
        if t == 0:
            value = partial(c, y_at(steps))
            for z in range(nz):
                rs_s[0, 0, c, z] = cut(value, z).astype(BF)
                for way in range(2):
                    rs_copy(way, 0, c, z).start()
            return
        values = [partial(c, y_at(steps - t)), partial(c, y_at(t - steps))]
        for z in range(nz):
            for way in range(2):
                value = cut(values[way], z)
                rs_copy(way, t - 1, c, z).wait_recv()
                if t == 1:
                    part = slice(0, half) if way == 0 else slice(half, rows)
                    rest = slice(half, rows) if way == 0 else slice(0, half)
                    rs_s[way, t, c, z, part] = (value[part] + rs_r[way, 0, c, z, part].astype(F32)).astype(BF)
                    rs_s[way, t, c, z, rest] = value[rest].astype(BF)
                else:
                    rs_s[way, t, c, z] = (value + rs_r[way, t - 1, c, z].astype(F32)).astype(BF)
                rs_copy(way, t, c, z).start()

    def rt_step(t):
        if t == 0:
            tails_t[...] = (mm(wtail[0], hid[...], 1, 1) + mm(wtail[1], gpr[...], 1, 1)).reshape(ny, 16, rows)
            rt_s[0, 0] = tails_t[y_at(steps)].astype(BF)
            rt_copy(0, 0).start()
            return
        for way in range(2):
            ends = tails_t[y_at(steps - t if way == 0 else t - steps)]
            if way == 0 or t > 1:
                rt_copy(way, t - 1).wait_recv()
                ends = ends + rt_r[way, t - 1].astype(F32)
            rt_s[way, t] = ends.astype(BF)
            rt_copy(way, t).start()

    def rs_last(c, value, z):
        for way in range(2):
            rs_copy(way, steps - 1, c, z).wait_recv()
        return cut(value, z) + rs_r[0, steps - 1, c, z].astype(F32) + rs_r[1, steps - 1, c, z].astype(F32)

    def s_copy(k, slot):
        return send(sbuf.at[me_d], sbuf.at[slot], s_ss.at[dp_at(k)], s_rs.at[slot], {"dp": dp_at(k)})

    def d1_copy(k, slot):
        return send(dr1.at[me_i], dr1.at[slot], d1_ss.at[inner_at(k)], d1_rs.at[slot], {"inner": inner_at(k)})

    def d2_copy(k, slot):
        return send(dro.at[me_x], dro.at[slot], d2_ss.at[outer_at(k)], d2_rs.at[slot], {"outer": outer_at(k)})

    def p3(c, peer, slot):
        s3, r3 = ((s3m, r3m), (s3t, r3t))[c]
        return send(s3.at[peer], r3.at[slot], p3_ss.at[c, peer], p3_rs.at[c, slot], {"outer": peer})

    def p4(c, z, peer, slot_z, slot_i):
        s4, r4 = ((s4m, r4m), (s4t, r4t))[c]
        return send(
            s4.at[z, peer], r4.at[slot_z, slot_i], p4_ss.at[c, z, peer], p4_rs.at[c, slot_z, slot_i],
            {"dp": z * ny + me_y, "inner": peer},
        )

    def p3_start(c):
        each(nx, lambda k: p3(c, outer_at(k), me_x).start())

    def p3_wait(c):
        each(nx, lambda k: p3(c, outer_at(k), outer_at(k)).wait())

    def p4_all(act):
        for dz in range(nz):
            z = lax.rem(me_z + dz, nz)
            each(ni, lambda k, z=z: act(z, inner_at(k)), 1 if dz == 0 else 0)

    def p4_start(c):
        p4_all(lambda z, peer: p4(c, z, peer, me_z, me_i).start())

    def p4_wait(c):
        p4_all(lambda z, peer: p4(c, z, peer, z, peer).wait())

    rs_step(0, 0)
    slope = 0.5 * (1.0 + tanh) + 0.5 * pre * (1.0 - tanh * tanh) * (
        root * (1.0 + (3.0 * cubic) * (pre * pre))
    )
    tails_scaled = (gate_col * tail_rows.astype(F32)).astype(BF)
    grad = mm(tails_scaled, wot[...], 1, 1)

    def scale_block(j, total):
        scaled = (gate_col * block(1, j).astype(F32)).astype(BF)
        scl[j] = scaled
        return total + mm(scaled, wo2[:, lanes_of(j)], 1, 1)

    grad = lax.fori_loop(0, ny, scale_block, grad)
    gpr[...] = (slope * grad).astype(BF)
    rs_step(0, 1)
    rs_step(1, 0)
    rt_step(0)
    product = hid[...].astype(F32) * grad
    dots = lax.dot_general(
        jnp.ones((8, ff), F32), product, (((1,), (1,)), ((), ())),
        precision=lax.Precision.HIGHEST, preferred_element_type=F32,
    )
    sbuf[me_d] = dots[0:1]
    each(ndp, lambda k: s_copy(k, me_d).start())
    for t in range(2, steps):
        rs_step(0, t)
    rs_step(1, 1)
    rt_step(1)

    value = partial(0, me_y)
    for z in range(nz):
        s3m[:, :, z * 128:(z + 1) * 128] = (gate_col * rs_last(0, value, z)).astype(BF).reshape(nx, rx, 128)
    p3_start(0)
    r3m[me_x] = s3m[me_x]
    for t in range(2, steps):
        rs_step(1, t)
        rt_step(t)
        if t == 2:
            each(ndp, lambda k: s_copy(k, dp_at(k)).wait())
            total = sbuf[0]
            for k in range(1, ndp):
                total = total + sbuf[k]
            xs[1:2, :] = total * (1.0 - gate_row)
    if steps < 3:
        each(ndp, lambda k: s_copy(k, dp_at(k)).wait())
        total = sbuf[0]
        for k in range(1, ndp):
            total = total + sbuf[k]
        xs[1:2, :] = total * (1.0 - gate_row)

    p3_wait(0)
    value = mm(swaps[1], r3m[...].reshape(rows, cb)).astype(BF)
    for z in range(nz):
        s4m[z] = value[:, z * 128:(z + 1) * 128].reshape(ni, ri, 128)
    p4_start(0)
    r4m[me_z, me_i] = s4m[me_z, me_i]

    lg_row = xs[1:2, :]
    lgs = stack3(lg_row)
    for j in range(ny):
        drn[:, j * cb:(j + 1) * cb] = jnp.broadcast_to(sum3(mm(lgs, block(0, j))), (8, cb))
    drn[:, mainw:] = jnp.broadcast_to(sum3(mm(lgs, tail_rows)), (8, 128))
    piece = drn[:, pl.ds(pl.multiple_of(me_d * 128, 128), 256)]
    dr1[me_i] = pltpu.roll(piece, lax.rem(256 - 2 * me_d, 256), 1)[0:1]
    each(ni, lambda k: d1_copy(k, me_i).start())
    rc = []
    for z in range(nz):
        d = z * ny + me_y
        piece = rvec[:, pl.ds(pl.multiple_of(d * 128, 128), 256)]
        mine = (me_z == z).astype(F32)
        rc.append(pltpu.roll(piece, lax.rem(256 - 2 * d, 256), 1)[0:1] * mine)

    value = partial(1, me_y)
    ends = tails_t[me_y]
    for way in range(2):
        rt_copy(way, steps - 1).wait_recv()
        ends = ends + rt_r[way, steps - 1].astype(F32)
    xs[8:24, :] = ends
    for q in range(2 * nz):
        xs[8 + q:9 + q, :] = xs[8 + q:9 + q, :] * gate_row
        z, k = q // 2, q % 2
        at = 8 + 2 * nz + q
        xs[at:at + 1, :] = xs[at:at + 1, :] + lg_row * rc[z][:, 128 + k:129 + k]
    turned = xs[...].T
    lg_col = turned[:, 1:2]
    s3t[:, :, cb:] = turned.astype(BF).reshape(nx, rx, 128)
    for z in range(nz):
        piece = rs_last(1, value, z) + lg_col * rc[z][:, :128]
        s3t[:, :, z * 128:(z + 1) * 128] = piece.astype(BF).reshape(nx, rx, 128)
    p3_start(1)
    r3t[me_x] = s3t[me_x]

    def weight_grads(j, carry):
        at = lanes_of(j)
        dwi[:, at] = mm(gpr[...], block(0, j), 0, 0).astype(BF)
        dwo[:, at] = mm(hid[...], scl[j], 0, 0).astype(BF)
        return carry

    each(ni, lambda k: d1_copy(k, inner_at(k)).wait())
    for k in range(ni):
        dro[me_x, k:k + 1] = dr1[k]
    each(nx, lambda k: d2_copy(k, me_x).start())
    lax.fori_loop(0, ny, weight_grads, 0)
    dwi[:, mainw:width] = mm(gpr[...], tail_rows, 0, 0)[:, :tw].astype(BF)
    dwo[:, mainw:width] = mm(hid[...], tails_scaled, 0, 0)[:, tw:2 * tw].astype(BF)

    p3_wait(1)
    value = mm(swaps[1], r3t[...].reshape(rows, cb + 128)).astype(BF)
    for z in range(nz):
        s4t[z, :, :, :128] = value[:, z * 128:(z + 1) * 128].reshape(ni, ri, 128)
        s4t[z, :, :, 128:] = value[:, cb:].reshape(ni, ri, 128)
    p4_start(1)
    r4t[me_z, me_i] = s4t[me_z, me_i]
    stores = [
        pltpu.make_async_copy(dwi, d_win.at[0], loc.at[7]),
        pltpu.make_async_copy(dwo, d_wout.at[0], loc.at[8]),
    ]
    for store in stores:
        store.start()

    def arrived(r4):
        value = r4[0].astype(F32)
        for z in range(1, nz):
            value = value + r4[z].astype(F32)
        return mm(value.astype(BF).reshape(rows, r4.shape[-1]), place_t[...], 0, 0)

    p4_wait(0)
    mixed[:128] = arrived(r4m).astype(BF)
    each(nx, lambda k: d2_copy(k, outer_at(k)).wait())
    drt[...] = dro[...].reshape(experts, 256)
    d_router[...] = drt[:, :per]

    for c in range(2):
        for way in range(2):
            for t in range(steps):
                ag_mine(c, way, t).wait_send()
                for z in range(nz):
                    rs_copy(way, t, c, z).wait_send()
    for way in range(2):
        for t in range(steps):
            if way == 0 or t > 0:
                rt_copy(way, t).wait_send()
    p4_wait(1)
    result = arrived(r4t)
    d_tok[:128] = result[:128].astype(BF)
    ends = result[136:138]
    more = result[136 + 2 * nz:138 + 2 * nz]
    for z in range(1, nz):
        at = 136 + 2 * z
        ends = jnp.where(me_z == z, result[at:at + 2], ends)
        more = jnp.where(me_z == z, result[at + 2 * nz:at + 2 * nz + 2], more)
    mixed[128:per] = ends.astype(BF)
    d_tok[128:per] = more.astype(BF)
    for store in stores:
        store.wait()


def on_device(nz, tokens, cotangent, expert_id, slot_id, router, w_in, w_out):
    ndp, nx, ni = lax.axis_size("dp"), lax.axis_size("outer"), lax.axis_size("inner")
    ny = ndp // nz
    steps = ny // 2
    tcount, width = tokens.shape
    experts = nx * ni
    rows = experts * CAP
    ri, rx = nx * CAP, ni * CAP
    cb = nz * 128
    padded = (ndp + 1) * 128
    per = width // ndp
    ff = w_in.shape[2]
    dma = pltpu.SemaphoreType.DMA
    vm = pltpu.VMEM
    scratch = [
        vm((cb, tcount), BF), vm((cb, tcount), BF), vm((128, tcount), BF), vm((ni, width), F32),
        vm((ff, width), BF), vm((ff, width), BF), vm((ff, width), BF), vm((ff, width), BF),
        vm((ni, ri, cb + 128), BF), vm((nx, rx, cb), BF), vm((ni, ri, cb + 128), BF), vm((nx, rx, cb), BF),
        vm((nx, rx, cb), BF), vm((nx, rx, 128), BF), vm((ni, ri, cb), BF), vm((ni, ri, cb), BF),
        vm((2, ny, nx, rx, cb), BF), vm((nx, rx, 128), BF), vm((ny, rows, cb), BF), vm((2, rows, rows), BF),
        vm((ff, padded), BF), vm((ff, padded), BF), vm((ff, 128), BF), vm((ny, ff, cb), BF), vm((ny, ff, cb), BF),
        vm((2, ny * 16, ff), BF), vm((8, padded), F32), vm((16, padded), BF), vm((rows, tcount), BF),
        vm((rows, ff), BF), vm((rows, ff), BF), vm((2, steps, 2, nz, rows, 128), BF), vm((2, steps, 2, nz, rows, 128), BF),
        vm((2, steps, 16, rows), BF), vm((2, steps, 16, rows), BF), vm((ny, 16, rows), F32), vm((128, rows), F32),
        vm((ndp, 1, rows), F32), vm((8, padded), F32), vm((ni, 1, 256), F32), vm((nx, ni, 256), F32), vm((experts, 256), F32),
        vm((nx, rx, cb), BF), vm((nx, rx, cb), BF), vm((nx, rx, cb + 128), BF), vm((nx, rx, cb + 128), BF),
        vm((nz, ni, ri, 128), BF), vm((nz, ni, ri, 128), BF), vm((nz, ni, ri, 256), BF), vm((nz, ni, ri, 256), BF),
        dma((9,)), dma((ni,)), dma((ni,)), dma((2, nx)), dma((2, nx)), dma((nx,)), dma((nx,)), dma((ni,)), dma((ni,)),
        dma((2, 2, steps)), dma((2, 2, steps)), dma((ndp,)), dma((ndp,)),
        dma((2, steps, 2, nz)), dma((2, steps, 2, nz)), dma((2, steps)), dma((2, steps)),
        dma((2, nx)), dma((2, nx)), dma((2, nz, ni)), dma((2, nz, ni)), dma((ni,)), dma((ni,)), dma((nx,)), dma((nx,)),
    ]
    shape = jax.ShapeDtypeStruct
    outs = pl.pallas_call(
        functools.partial(kernel, nz),
        out_shape=(
            shape((per, tcount), BF), shape((per, tcount), BF),
            shape(w_out.shape, BF), shape(w_out.shape, BF), shape((experts, per), F32),
        ),
        in_specs=[pl.BlockSpec(memory_space=pltpu.VMEM)] * 2 + [pl.BlockSpec(memory_space=pl.ANY)] * 5,
        out_specs=tuple(
            pl.BlockSpec(memory_space=space)
            for space in (pltpu.VMEM, pltpu.VMEM, pl.ANY, pl.ANY, pltpu.VMEM)
        ),
        scratch_shapes=scratch,
        compiler_params=pltpu.CompilerParams(
            collective_id=0, has_side_effects=True, vmem_limit_bytes=VMEM_LIMIT
        ),
    )(
        expert_id.reshape(1, tcount), slot_id.reshape(1, tcount), tokens.T, cotangent.T, router.T,
        jnp.swapaxes(w_in, 1, 2), w_out,
    )
    mixed, d_tok, d_win, d_wout, d_router = outs
    return mixed.T, d_tok.T, jnp.swapaxes(d_win, 1, 2), d_wout, d_router.T


def build(mesh, nz):
    return jax.shard_map(
        functools.partial(on_device, nz),
        mesh=mesh,
        in_specs=(
            P(("outer", "inner"), None),
            P(("outer", "inner"), None),
            P(("outer", "inner")),
            P(("outer", "inner")),
            P(),
            P(("outer", "inner"), None, "dp"),
            P(("outer", "inner"), "dp", None),
        ),
        out_specs=(
            P(("outer", "inner"), "dp"),
            P(("outer", "inner"), "dp"),
            P(("outer", "inner"), None, "dp"),
            P(("outer", "inner"), "dp", None),
            P("dp", None),
        ),
        check_vma=False,
    )


def solution(mesh):
    return build(mesh, NZ)
```

```python
import functools

import jax
import jax.numpy as jnp
from jax import lax
from jax.experimental import pallas as pl
from jax.experimental.pallas import tpu as pltpu
from jax.sharding import PartitionSpec as P

BF = jnp.bfloat16
F32 = jnp.float32
NZ = 2
CAP = 4
VMEM_LIMIT = 60 * 1024 * 1024


def mm(a, b, ca=1, cb=0):
    return lax.dot_general(a, b, (((ca,), (cb,)), ((), ())), preferred_element_type=F32)


def split3(value):
    hi = value.astype(BF)
    rest = value - hi.astype(F32)
    mid = rest.astype(BF)
    low = (rest - mid.astype(F32)).astype(BF)
    return hi, mid, low


def stack3(value):
    hi, mid, low = (part.astype(F32) for part in split3(value[0:1]))
    row = lax.broadcasted_iota(jnp.int32, (16, value.shape[1]), 0)
    out = jnp.where(row == 0, hi, jnp.where(row == 1, mid, jnp.where(row == 2, low, 0.0)))
    return out.astype(BF)


def sum3(value):
    return value[0:1] + (value[1:2] + value[2:3])


def iota(shape, dim):
    return lax.broadcasted_iota(jnp.int32, shape, dim)


def log2(value):
    return value.bit_length() - 1


def kernel(
    nz,
    eid, sid, tokens, cot, router, w_in, w_out,
    mixed, d_tok, d_win, d_wout, d_router,
    tokx, cotx, ends_t, rrow, wir, wor, dwi, dwo,
    s1a, s1b, r1a, r1b, s2a, s2t, s2b, r2b, main, tail, scl, swaps,
    wi2, wo2, wot, wip, wop, wtail, rvec, rpart, place_t,
    hid, gpr, rs_s, rs_r, rt_s, rt_r, tails_t, xs,
    sbuf, drn, dr1, dro, drt, s3m, r3m, s3t, r3t, s4m, r4m, s4t, r4t,
    loc, a1_ss, a1_rs, a2_ss, a2_rs, b1_ss, b1_rs, b2_ss, b2_rs,
    ag_ss, ag_rs, s_ss, s_rs, rm_ss, rm_rs, rt_ss, rt_rs,
    p3_ss, p3_rs, p4_ss, p4_rs, d1_ss, d1_rs, d2_ss, d2_rs,
):
    ndp, nx, ni = lax.axis_size("dp"), lax.axis_size("outer"), lax.axis_size("inner")
    ny = ndp // nz
    me_d, me_x, me_i = lax.axis_index("dp"), lax.axis_index("outer"), lax.axis_index("inner")
    me_y, me_z = lax.rem(me_d, ny), lax.div(me_d, ny)
    steps = ny // 2
    width, tcount = tokens.shape
    experts = nx * ni
    rows = experts * CAP
    ri, rx = nx * CAP, ni * CAP
    cb = nz * 128
    mainw = ndp * 128
    tw = width - mainw
    per = width // ndp
    ff = hid.shape[1]
    right, left = lax.rem(me_y + 1, ny), lax.rem(me_y + ny - 1, ny)
    half = rows // 2

    def send(src, dst, ss, rs, where):
        return pltpu.make_async_remote_copy(
            src_ref=src, dst_ref=dst, send_sem=ss, recv_sem=rs,
            device_id=where, device_id_type=pl.DeviceIdType.MESH,
        )

    def each(count, body, first=1):
        def step(k, carry):
            body(k)
            return carry

        lax.fori_loop(first, count, step, 0)

    def inner_at(k):
        return lax.rem(me_i + k, ni)

    def outer_at(k):
        return lax.rem(me_x + k, nx)

    def dp_at(k):
        return lax.rem(me_d + k, ndp)

    def y_at(k):
        return lax.rem(me_y + ny + k, ny)

    def far_dp(dz):
        return lax.rem(me_z + dz, nz) * ny + me_y

    def block(c, j):
        return main[c, j].reshape(rows, cb)

    def lanes_of(j):
        return pl.ds(pl.multiple_of(j * cb, 128), cb)

    barrier = pltpu.get_barrier_semaphore()

    def hello(where):
        pl.semaphore_signal(barrier, inc=1, device_id=where, device_id_type=pl.DeviceIdType.MESH)

    each(ni, lambda k: hello({"inner": inner_at(k)}))
    each(nx, lambda k: hello({"outer": outer_at(k)}))
    each(ndp, lambda k: hello({"dp": dp_at(k)}))
    for dz in range(1, nz):
        each(ni, lambda k, dz=dz: hello({"dp": far_dp(dz), "inner": inner_at(k)}))

    own = lanes_of(me_y)
    loads = [
        pltpu.make_async_copy(src, dst, loc.at[i])
        for i, (src, dst) in enumerate((
            (tokens.at[own], tokx),
            (tokens.at[pl.ds(mainw, tw)], ends_t.at[pl.ds(0, tw)]),
            (cot.at[pl.ds(mainw, tw)], ends_t.at[pl.ds(tw, tw)]),
            (cot.at[own], cotx),
            (router.at[pl.ds(pl.multiple_of(me_x * ni, ni), ni)], rrow),
            (w_in.at[0], wir),
            (w_out.at[0], wor),
        ))
    ]
    for load in loads:
        load.start()

    e, s = eid[...], sid[...]
    place_t[...] = (iota((rows, tcount), 0) == jnp.where(s >= 0, e * CAP + s, -1)).astype(BF)
    ends_t[2 * tw:] = jnp.zeros((128 - 2 * tw, tcount), BF)
    for load in loads[:3]:
        load.wait()
    s1a[:, :, :cb] = mm(place_t[...], tokx[...], 1, 1).astype(BF).reshape(nx, rx, cb)
    s1a[:, :, cb:] = mm(place_t[...], ends_t[...], 1, 1).astype(BF).reshape(nx, rx, 128)
    pl.semaphore_wait(barrier, (ni - 1) * nz + (nx - 1) + (ndp - 1))

    def a1(peer, slot):
        return send(s1a.at[peer], r1a.at[slot], a1_ss.at[peer], a1_rs.at[slot], {"outer": peer})

    def b1(peer, slot):
        return send(s1b.at[peer], r1b.at[slot], b1_ss.at[peer], b1_rs.at[slot], {"inner": peer})

    each(nx, lambda k: a1(outer_at(k), me_x).start())
    spot = jnp.where(s >= 0, (e & (ni - 1)) * ri + (e >> log2(ni)) * CAP + s, -1)
    place_b = (iota((rows, tcount), 0) == spot).astype(BF)
    loads[3].wait()
    s1b[...] = mm(place_b, cotx[...], 1, 1).astype(BF).reshape(ni, ri, cb)
    each(ni, lambda k: b1(inner_at(k), me_i).start())
    r1a[me_x] = s1a[me_x]
    r1b[me_i] = s1b[me_i]

    row, col = iota((rows, rows), 0), iota((rows, rows), 1)
    same_slot = (row & (CAP - 1)) == (col & (CAP - 1))
    row4, col4 = row >> log2(CAP), col >> log2(CAP)
    to_outer, to_inner = 0, 1
    swaps[to_outer] = (
        same_slot
        & ((row4 >> log2(ni)) == (col4 & (nx - 1)))
        & ((row4 & (ni - 1)) == (col4 >> log2(nx)))
    ).astype(BF)
    swaps[to_inner] = (
        same_slot
        & ((row4 >> log2(nx)) == (col4 & (ni - 1)))
        & ((row4 & (nx - 1)) == (col4 >> log2(ni)))
    ).astype(BF)

    def a2(q, peer, slot):
        src = (s2a if q == 0 else s2t).at[peer]
        dst = main.at[0, me_y, slot] if q == 0 else tail.at[slot]
        return send(src, dst, a2_ss.at[q, peer], a2_rs.at[q, slot], {"inner": peer})

    def b2(peer, slot):
        return send(s2b.at[peer], r2b.at[slot], b2_ss.at[peer], b2_rs.at[slot], {"outer": peer})

    each(nx, lambda k: a1(outer_at(k), outer_at(k)).wait())
    s2a[...] = mm(swaps[to_inner], r1a[:, :, :cb].reshape(rows, cb)).astype(BF).reshape(ni, ri, cb)
    each(ni, lambda k: a2(0, inner_at(k), me_i).start())
    s2t[...] = mm(swaps[to_inner], r1a[:, :, cb:].reshape(rows, 128)).astype(BF).reshape(ni, ri, 128)
    each(ni, lambda k: a2(1, inner_at(k), me_i).start())
    each(ni, lambda k: b1(inner_at(k), inner_at(k)).wait())
    s2b[...] = mm(swaps[to_outer], r1b[...].reshape(rows, cb)).astype(BF).reshape(nx, rx, cb)
    each(nx, lambda k: b2(outer_at(k), me_x).start())
    main[0, me_y, me_i] = s2a[me_i]
    tail[me_i] = s2t[me_i]
    r2b[me_x] = s2b[me_x]

    for load in loads[4:]:
        load.wait()
    rvec[:, :width] = jnp.broadcast_to(rrow[pl.ds(me_i, 1), :], (8, width))
    rvec[:, width:] = jnp.zeros((8, rvec.shape[1] - width), F32)
    wi2[:, :width] = wir[...]
    wi2[:, width:] = jnp.zeros((ff, wi2.shape[1] - width), BF)
    wo2[:, :width] = wor[...]
    wo2[:, width:] = jnp.zeros((ff, wo2.shape[1] - width), BF)

    def ag(c, way, t, j):
        ref = main.at[c, j]
        if t == steps - 1:
            ref = main.at[c, j, pl.ds(0 if way == 0 else ni // 2, ni // 2)]
        peer = right if way == 0 else left
        return send(ref, ref, ag_ss.at[c, way, t], ag_rs.at[c, way, t], {"dp": me_z * ny + peer})

    def ag_mine(c, way, t):
        return ag(c, way, t, y_at(-t if way == 0 else t))

    def ag_theirs(c, way, t):
        return ag(c, way, t, y_at(-t - 1 if way == 0 else t + 1))

    each(ni, lambda k: a2(0, inner_at(k), inner_at(k)).wait())
    for way in range(2):
        ag_mine(0, way, 0).start()
    each(nx, lambda k: b2(outer_at(k), outer_at(k)).wait())
    main[1, me_y] = mm(swaps[to_inner], r2b[...].reshape(rows, cb)).astype(BF).reshape(ni, ri, cb)
    for way in range(2):
        ag_mine(1, way, 0).start()
    each(ni, lambda k: a2(1, inner_at(k), inner_at(k)).wait())

    def reorder(d, carry):
        y, z = lax.rem(d, ny), lax.div(d, ny)
        at = pl.ds(pl.multiple_of(d * 128, 128), 256)
        part = pl.ds(pl.multiple_of(z * 128, 128), 128)
        pick = (iota((256, 128), 0) == iota((256, 128), 1) + 2 * d).astype(BF)
        wop[y, :, part] = mm(wo2[:, at], pick).astype(BF)
        wip[y, :, part] = mm(wi2[:, at], pick).astype(BF)
        return carry

    def tail_weights():
        shape = (ny * 16, wo2.shape[1])
        q, y = iota(shape, 0) & 15, iota(shape, 0) >> 4
        for first, ref in ((0, wo2), (2 * nz, wi2)):
            qq = q - first
            want = ((qq >> 1) * ny + y) * per + 128 + (qq & 1)
            pick = ((want == iota(shape, 1)) & (qq >= 0) & (qq < 2 * nz)).astype(BF)
            wtail[0 if first == 0 else 1] = mm(pick, ref[...], 1, 1).astype(BF)

    rpart[...] = stack3(rvec[...])
    tail_rows = tail[...].reshape(rows, 128)
    pre = mm(tail_rows, wi2[:, mainw:], 1, 1)
    lg3 = mm(rpart[:, mainw:], tail_rows, 1, 1)

    def forward_block(j, pre, lg3):
        at = lanes_of(j)
        return (
            pre + mm(block(0, j), wi2[:, at], 1, 1),
            lg3 + mm(rpart[:, at], block(0, j), 1, 1),
        )

    pre, lg3 = forward_block(me_y, pre, lg3)
    wot[...] = mm(
        wo2[:, mainw:],
        ((iota((128, 128), 0) + tw == iota((128, 128), 1)) & (iota((128, 128), 0) < tw)).astype(BF),
    ).astype(BF)
    for t in range(1, steps + 1):
        for c in range(2 if t < steps else 1):
            for way in range(2):
                ag_theirs(c, way, t - 1).wait_recv()
                if t < steps:
                    ag_mine(c, way, t).start()
            if c == 0:
                pre, lg3 = forward_block(y_at(t), pre, lg3)
                if t < steps:
                    pre, lg3 = forward_block(y_at(-t), pre, lg3)
                    many = -(-ndp // (steps - 1))
                    lax.fori_loop((t - 1) * many, min(ndp, t * many), reorder, 0)
        if t == 1:
            tail_weights()

    gate_row = jax.nn.sigmoid(sum3(lg3))
    xs[...] = jnp.zeros(xs.shape, F32)
    xs[0:1, :] = gate_row
    gate_col = xs[...].T[:, 0:1]
    root, cubic = 0.7978845608028654, 0.044715
    tanh = jnp.tanh(root * (pre + cubic * (pre * pre * pre)))
    hid[...] = (0.5 * pre * (1.0 + tanh)).astype(BF)

    def rs_copy(way, t, c, z):
        src, dst = rs_s.at[way, t, c, z], rs_r.at[way, t, c, z]
        if t == 0:
            part = pl.ds(0 if way == 0 else half, half)
            src, dst = rs_s.at[0, 0, c, z, part], rs_r.at[way, 0, c, z, part]
        peer = right if way == 0 else left
        return send(src, dst, rm_ss.at[way, t, c, z], rm_rs.at[way, t, c, z], {"dp": me_z * ny + peer})

    def rt_copy(way, t):
        peer = right if way == 0 else left
        return send(rt_s.at[way, t], rt_r.at[way, t], rt_ss.at[way, t], rt_rs.at[way, t], {"dp": me_z * ny + peer})

    def partial(c, b):
        return mm(hid[...], wop[b]) if c == 0 else mm(gpr[...], wip[b])

    def cut(value, z):
        return value[:, z * 128:(z + 1) * 128]

    def rs_step(c, t):
        if t == 0:
            value = partial(c, y_at(steps))
            for z in range(nz):
                rs_s[0, 0, c, z] = cut(value, z).astype(BF)
                for way in range(2):
                    rs_copy(way, 0, c, z).start()
            return
        values = [partial(c, y_at(steps - t)), partial(c, y_at(t - steps))]
        for z in range(nz):
            for way in range(2):
                value = cut(values[way], z)
                rs_copy(way, t - 1, c, z).wait_recv()
                if t == 1:
                    part = slice(0, half) if way == 0 else slice(half, rows)
                    rest = slice(half, rows) if way == 0 else slice(0, half)
                    rs_s[way, t, c, z, part] = (value[part] + rs_r[way, 0, c, z, part].astype(F32)).astype(BF)
                    rs_s[way, t, c, z, rest] = value[rest].astype(BF)
                else:
                    rs_s[way, t, c, z] = (value + rs_r[way, t - 1, c, z].astype(F32)).astype(BF)
                rs_copy(way, t, c, z).start()

    def rt_step(t):
        if t == 0:
            tails_t[...] = (mm(wtail[0], hid[...], 1, 1) + mm(wtail[1], gpr[...], 1, 1)).reshape(ny, 16, rows)
            rt_s[0, 0] = tails_t[y_at(steps)].astype(BF)
            rt_copy(0, 0).start()
            return
        for way in range(2):
            ends = tails_t[y_at(steps - t if way == 0 else t - steps)]
            if way == 0 or t > 1:
                rt_copy(way, t - 1).wait_recv()
                ends = ends + rt_r[way, t - 1].astype(F32)
            rt_s[way, t] = ends.astype(BF)
            rt_copy(way, t).start()

    def rs_last(c, value, z):
        for way in range(2):
            rs_copy(way, steps - 1, c, z).wait_recv()
        return cut(value, z) + rs_r[0, steps - 1, c, z].astype(F32) + rs_r[1, steps - 1, c, z].astype(F32)

    def s_copy(k, slot):
        return send(sbuf.at[me_d], sbuf.at[slot], s_ss.at[dp_at(k)], s_rs.at[slot], {"dp": dp_at(k)})

    def d1_copy(k, slot):
        return send(dr1.at[me_i], dr1.at[slot], d1_ss.at[inner_at(k)], d1_rs.at[slot], {"inner": inner_at(k)})

    def d2_copy(k, slot):
        return send(dro.at[me_x], dro.at[slot], d2_ss.at[outer_at(k)], d2_rs.at[slot], {"outer": outer_at(k)})

    def p3(c, peer, slot):
        s3, r3 = ((s3m, r3m), (s3t, r3t))[c]
        return send(s3.at[peer], r3.at[slot], p3_ss.at[c, peer], p3_rs.at[c, slot], {"outer": peer})

    def p4(c, z, peer, slot_z, slot_i):
        s4, r4 = ((s4m, r4m), (s4t, r4t))[c]
        return send(
            s4.at[z, peer], r4.at[slot_z, slot_i], p4_ss.at[c, z, peer], p4_rs.at[c, slot_z, slot_i],
            {"dp": z * ny + me_y, "inner": peer},
        )

    def p3_start(c):
        each(nx, lambda k: p3(c, outer_at(k), me_x).start())

    def p3_wait(c):
        each(nx, lambda k: p3(c, outer_at(k), outer_at(k)).wait())

    def p4_all(act):
        for dz in range(nz):
            z = lax.rem(me_z + dz, nz)
            each(ni, lambda k, z=z: act(z, inner_at(k)), 1 if dz == 0 else 0)

    def p4_start(c):
        p4_all(lambda z, peer: p4(c, z, peer, me_z, me_i).start())

    def p4_wait(c):
        p4_all(lambda z, peer: p4(c, z, peer, z, peer).wait())

    rs_step(0, 0)
    for way in range(2):
        ag_theirs(1, way, steps - 1).wait_recv()
    slope = 0.5 * (1.0 + tanh) + 0.5 * pre * (1.0 - tanh * tanh) * (
        root * (1.0 + (3.0 * cubic) * (pre * pre))
    )
    tails_scaled = (gate_col * tail_rows.astype(F32)).astype(BF)
    grad = mm(tails_scaled, wot[...], 1, 1)

    def scale_block(j, total):
        scaled = (gate_col * block(1, j).astype(F32)).astype(BF)
        scl[j] = scaled
        return total + mm(scaled, wo2[:, lanes_of(j)], 1, 1)

    grad = lax.fori_loop(0, ny, scale_block, grad)
    gpr[...] = (slope * grad).astype(BF)
    rs_step(1, 0)
    rt_step(0)
    rs_step(0, 1)
    product = hid[...].astype(F32) * grad
    dots = lax.dot_general(
        jnp.ones((8, ff), F32), product, (((1,), (1,)), ((), ())),
        precision=lax.Precision.HIGHEST, preferred_element_type=F32,
    )
    sbuf[me_d] = dots[0:1]
    each(ndp, lambda k: s_copy(k, me_d).start())
    for t in range(1, steps):
        rs_step(1, t)
        rt_step(t)
        if t == steps - 2:
            each(ndp, lambda k: s_copy(k, dp_at(k)).wait())
            total = sbuf[0]
            for k in range(1, ndp):
                total = total + sbuf[k]
            xs[1:2, :] = total * (1.0 - gate_row)
        if t < steps - 1:
            rs_step(0, t + 1)
    if steps < 3:
        each(ndp, lambda k: s_copy(k, dp_at(k)).wait())
        total = sbuf[0]
        for k in range(1, ndp):
            total = total + sbuf[k]
        xs[1:2, :] = total * (1.0 - gate_row)

    value = partial(0, me_y)
    for z in range(nz):
        s4m[z] = (gate_col * rs_last(0, value, z)).astype(BF).reshape(ni, ri, 128)
    p4_start(0)
    r4m[me_z, me_i] = s4m[me_z, me_i]

    lg_row = xs[1:2, :]
    lgs = stack3(lg_row)
    for j in range(ny):
        drn[:, j * cb:(j + 1) * cb] = jnp.broadcast_to(sum3(mm(lgs, block(0, j))), (8, cb))
    drn[:, mainw:] = jnp.broadcast_to(sum3(mm(lgs, tail_rows)), (8, 128))
    piece = drn[:, pl.ds(pl.multiple_of(me_d * 128, 128), 256)]
    dr1[me_i] = pltpu.roll(piece, lax.rem(256 - 2 * me_d, 256), 1)[0:1]
    each(ni, lambda k: d1_copy(k, me_i).start())
    rc = []
    for z in range(nz):
        d = z * ny + me_y
        piece = rvec[:, pl.ds(pl.multiple_of(d * 128, 128), 256)]
        mine = (me_z == z).astype(F32)
        rc.append(pltpu.roll(piece, lax.rem(256 - 2 * d, 256), 1)[0:1] * mine)

    value = partial(1, me_y)
    ends = tails_t[me_y]
    for way in range(2):
        rt_copy(way, steps - 1).wait_recv()
        ends = ends + rt_r[way, steps - 1].astype(F32)
    xs[8:24, :] = ends
    for q in range(2 * nz):
        xs[8 + q:9 + q, :] = xs[8 + q:9 + q, :] * gate_row
        z, k = q // 2, q % 2
        at = 8 + 2 * nz + q
        xs[at:at + 1, :] = xs[at:at + 1, :] + lg_row * rc[z][:, 128 + k:129 + k]
    turned = xs[...].T
    lg_col = turned[:, 1:2]
    ends = turned.astype(BF).reshape(ni, ri, 128)
    for z in range(nz):
        piece = rs_last(1, value, z) + lg_col * rc[z][:, :128]
        s4t[z, :, :, :128] = piece.astype(BF).reshape(ni, ri, 128)
        s4t[z, :, :, 128:] = ends
    p4_start(1)
    r4t[me_z, me_i] = s4t[me_z, me_i]

    def onward(c):
        r4, s3, r3 = ((r4m, s3m, r3m), (r4t, s3t, r3t))[c]
        p4_wait(c)
        value = r4[0].astype(F32)
        for z in range(1, nz):
            value = value + r4[z].astype(F32)
        value = value.astype(BF).reshape(rows, r4.shape[-1])
        s3[...] = mm(swaps[to_outer], value).astype(BF).reshape(s3.shape)
        p3_start(c)
        r3[me_x] = s3[me_x]

    onward(0)

    def weight_grads(j, carry):
        at = lanes_of(j)
        dwi[:, at] = mm(gpr[...], block(0, j), 0, 0).astype(BF)
        dwo[:, at] = mm(hid[...], scl[j], 0, 0).astype(BF)
        return carry

    each(ni, lambda k: d1_copy(k, inner_at(k)).wait())
    for k in range(ni):
        dro[me_x, k:k + 1] = dr1[k]
    each(nx, lambda k: d2_copy(k, me_x).start())
    lax.fori_loop(0, ny, weight_grads, 0)
    dwi[:, mainw:width] = mm(gpr[...], tail_rows, 0, 0)[:, :tw].astype(BF)
    dwo[:, mainw:width] = mm(hid[...], tails_scaled, 0, 0)[:, tw:2 * tw].astype(BF)

    onward(1)
    stores = [
        pltpu.make_async_copy(dwi, d_win.at[0], loc.at[7]),
        pltpu.make_async_copy(dwo, d_wout.at[0], loc.at[8]),
    ]
    for store in stores:
        store.start()

    def arrived(r3):
        return mm(r3[...].reshape(rows, r3.shape[-1]), place_t[...], 0, 0)

    p3_wait(0)
    mixed[:128] = arrived(r3m).astype(BF)
    each(nx, lambda k: d2_copy(k, outer_at(k)).wait())
    drt[...] = dro[...].reshape(experts, 256)
    d_router[...] = drt[:, :per]

    for c in range(2):
        for way in range(2):
            for t in range(steps):
                ag_mine(c, way, t).wait_send()
                for z in range(nz):
                    rs_copy(way, t, c, z).wait_send()
    for way in range(2):
        for t in range(steps):
            if way == 0 or t > 0:
                rt_copy(way, t).wait_send()
    p3_wait(1)
    result = arrived(r3t)
    d_tok[:128] = result[:128].astype(BF)
    ends = result[136:138]
    more = result[136 + 2 * nz:138 + 2 * nz]
    for z in range(1, nz):
        at = 136 + 2 * z
        ends = jnp.where(me_z == z, result[at:at + 2], ends)
        more = jnp.where(me_z == z, result[at + 2 * nz:at + 2 * nz + 2], more)
    mixed[128:per] = ends.astype(BF)
    d_tok[128:per] = more.astype(BF)
    for store in stores:
        store.wait()


def store(*refs):
    ins, outs, held, sems = refs[:5], refs[5:10], refs[10:15], refs[15]
    loads = [pltpu.make_async_copy(ins[i], held[i], sems.at[0, i]) for i in range(5)]
    stores = [pltpu.make_async_copy(held[i], outs[i], sems.at[1, i]) for i in range(5)]
    for copy in loads:
        copy.start()
    for load, copy in zip(loads, stores):
        load.wait()
        copy.start()
    for copy in stores:
        copy.wait()


def on_device(nz, tokens, cotangent, expert_id, slot_id, router, w_in, w_out):
    ndp, nx, ni = lax.axis_size("dp"), lax.axis_size("outer"), lax.axis_size("inner")
    ny = ndp // nz
    steps = ny // 2
    tcount, width = tokens.shape
    experts = nx * ni
    rows = experts * CAP
    ri, rx = nx * CAP, ni * CAP
    cb = nz * 128
    padded = (ndp + 1) * 128
    per = width // ndp
    ff = w_in.shape[2]
    dma = pltpu.SemaphoreType.DMA
    vm = pltpu.VMEM
    scratch = [
        vm((cb, tcount), BF), vm((cb, tcount), BF), vm((128, tcount), BF), vm((ni, width), F32),
        vm((ff, width), BF), vm((ff, width), BF), vm((ff, width), BF), vm((ff, width), BF),
        vm((nx, rx, cb + 128), BF), vm((ni, ri, cb), BF), vm((nx, rx, cb + 128), BF), vm((ni, ri, cb), BF),
        vm((ni, ri, cb), BF), vm((ni, ri, 128), BF), vm((nx, rx, cb), BF), vm((nx, rx, cb), BF),
        vm((2, ny, ni, ri, cb), BF), vm((ni, ri, 128), BF), vm((ny, rows, cb), BF), vm((2, rows, rows), BF),
        vm((ff, padded), BF), vm((ff, padded), BF), vm((ff, 128), BF), vm((ny, ff, cb), BF), vm((ny, ff, cb), BF),
        vm((2, ny * 16, ff), BF), vm((8, padded), F32), vm((16, padded), BF), vm((rows, tcount), BF),
        vm((rows, ff), BF), vm((rows, ff), BF), vm((2, steps, 2, nz, rows, 128), BF), vm((2, steps, 2, nz, rows, 128), BF),
        vm((2, steps, 16, rows), BF), vm((2, steps, 16, rows), BF), vm((ny, 16, rows), F32), vm((128, rows), F32),
        vm((ndp, 1, rows), F32), vm((8, padded), F32), vm((ni, 1, 256), F32), vm((nx, ni, 256), F32), vm((experts, 256), F32),
        vm((nx, rx, 128), BF), vm((nx, rx, 128), BF), vm((nx, rx, 256), BF), vm((nx, rx, 256), BF),
        vm((nz, ni, ri, 128), BF), vm((nz, ni, ri, 128), BF), vm((nz, ni, ri, 256), BF), vm((nz, ni, ri, 256), BF),
        dma((9,)), dma((nx,)), dma((nx,)), dma((2, ni)), dma((2, ni)), dma((ni,)), dma((ni,)), dma((nx,)), dma((nx,)),
        dma((2, 2, steps)), dma((2, 2, steps)), dma((ndp,)), dma((ndp,)),
        dma((2, steps, 2, nz)), dma((2, steps, 2, nz)), dma((2, steps)), dma((2, steps)),
        dma((2, nx)), dma((2, nx)), dma((2, nz, ni)), dma((2, nz, ni)), dma((ni,)), dma((ni,)), dma((nx,)), dma((nx,)),
    ]
    shape = jax.ShapeDtypeStruct
    outs = pl.pallas_call(
        functools.partial(kernel, nz),
        out_shape=(
            shape((per, tcount), BF), shape((per, tcount), BF),
            shape(w_out.shape, BF), shape(w_out.shape, BF), shape((experts, per), F32),
        ),
        in_specs=[pl.BlockSpec(memory_space=pltpu.VMEM)] * 2 + [pl.BlockSpec(memory_space=pl.ANY)] * 5,
        out_specs=tuple(
            pl.BlockSpec(memory_space=space)
            for space in (pltpu.VMEM, pltpu.VMEM, pl.ANY, pl.ANY, pltpu.VMEM)
        ),
        scratch_shapes=scratch,
        compiler_params=pltpu.CompilerParams(
            collective_id=0, has_side_effects=True, vmem_limit_bytes=VMEM_LIMIT
        ),
    )(
        expert_id.reshape(1, tcount), slot_id.reshape(1, tcount), tokens.T, cotangent.T, router.T,
        jnp.swapaxes(w_in, 1, 2), w_out,
    )
    mixed, d_tok, d_win, d_wout, d_router = pl.pallas_call(
        store,
        out_shape=tuple(shape(out.shape, out.dtype) for out in outs),
        in_specs=[pl.BlockSpec(memory_space=pl.ANY)] * 5,
        out_specs=tuple([pl.BlockSpec(memory_space=pl.ANY)] * 5),
        scratch_shapes=[vm(out.shape, out.dtype) for out in outs] + [dma((2, 5))],
        compiler_params=pltpu.CompilerParams(vmem_limit_bytes=VMEM_LIMIT),
    )(*outs)
    return mixed.T, d_tok.T, jnp.swapaxes(d_win, 1, 2), d_wout, d_router.T


def build(mesh, nz):
    return jax.shard_map(
        functools.partial(on_device, nz),
        mesh=mesh,
        in_specs=(
            P(("outer", "inner"), None),
            P(("outer", "inner"), None),
            P(("outer", "inner")),
            P(("outer", "inner")),
            P(),
            P(("outer", "inner"), None, "dp"),
            P(("outer", "inner"), "dp", None),
        ),
        out_specs=(
            P(("outer", "inner"), "dp"),
            P(("outer", "inner"), "dp"),
            P(("outer", "inner"), None, "dp"),
            P(("outer", "inner"), "dp", None),
            P("dp", None),
        ),
        check_vma=False,
    )


def solution(mesh):
    return build(mesh, NZ)
```

```python
import functools

import jax
import jax.numpy as jnp
from jax import lax
from jax.experimental import pallas as pl
from jax.experimental.pallas import tpu as pltpu
from jax.sharding import PartitionSpec as P

BF = jnp.bfloat16
F32 = jnp.float32
NZ = 2
CAP = 4
VMEM_LIMIT = 60 * 1024 * 1024


def mm(a, b, ca=1, cb=0):
    return lax.dot_general(a, b, (((ca,), (cb,)), ((), ())), preferred_element_type=F32)


def split3(value):
    hi = value.astype(BF)
    rest = value - hi.astype(F32)
    mid = rest.astype(BF)
    low = (rest - mid.astype(F32)).astype(BF)
    return hi, mid, low


def stack3(value):
    hi, mid, low = (part.astype(F32) for part in split3(value[0:1]))
    row = lax.broadcasted_iota(jnp.int32, (16, value.shape[1]), 0)
    out = jnp.where(row == 0, hi, jnp.where(row == 1, mid, jnp.where(row == 2, low, 0.0)))
    return out.astype(BF)


def sum3(value):
    return value[0:1] + (value[1:2] + value[2:3])


def iota(shape, dim):
    return lax.broadcasted_iota(jnp.int32, shape, dim)


def log2(value):
    return value.bit_length() - 1


def kernel(
    nz,
    eid, sid, tokens, cot, router, w_in, w_out,
    mixed, d_tok, d_win, d_wout, d_router,
    tokx, cotx, ends_t, rrow, wir, wor, dwi, dwo,
    s1a, s1b, r1a, r1b, s2a, s2t, s2b, r2b, main, tail, scl, swaps,
    wi2, wo2, wot, wip, wop, wtail, rvec, rpart, place_t,
    hid, gpr, rs_s, rs_r, rt_s, rt_r, tails_t, xs,
    sbuf, drn, dr1, dro, drt, s3m, r3m, s3t, r3t, s4m, r4m, s4t, r4t,
    loc, a1_ss, a1_rs, a2_ss, a2_rs, b1_ss, b1_rs, b2_ss, b2_rs,
    ag_ss, ag_rs, s_ss, s_rs, rm_ss, rm_rs, rt_ss, rt_rs,
    p3_ss, p3_rs, p4_ss, p4_rs, d1_ss, d1_rs, d2_ss, d2_rs,
):
    ndp, nx, ni = lax.axis_size("dp"), lax.axis_size("outer"), lax.axis_size("inner")
    ny = ndp // nz
    me_d, me_x, me_i = lax.axis_index("dp"), lax.axis_index("outer"), lax.axis_index("inner")
    me_y, me_z = lax.rem(me_d, ny), lax.div(me_d, ny)
    steps = ny // 2
    width, tcount = tokens.shape
    experts = nx * ni
    rows = experts * CAP
    ri, rx = nx * CAP, ni * CAP
    cb = nz * 128
    mainw = ndp * 128
    tw = width - mainw
    per = width // ndp
    ff = hid.shape[1]
    right, left = lax.rem(me_y + 1, ny), lax.rem(me_y + ny - 1, ny)
    half = rows // 2

    def send(src, dst, ss, rs, where):
        return pltpu.make_async_remote_copy(
            src_ref=src, dst_ref=dst, send_sem=ss, recv_sem=rs,
            device_id=where, device_id_type=pl.DeviceIdType.MESH,
        )

    def each(count, body, first=1):
        def step(k, carry):
            body(k)
            return carry

        lax.fori_loop(first, count, step, 0)

    def inner_at(k):
        return lax.rem(me_i + k, ni)

    def outer_at(k):
        return lax.rem(me_x + k, nx)

    def dp_at(k):
        return lax.rem(me_d + k, ndp)

    def y_at(k):
        return lax.rem(me_y + ny + k, ny)

    def far_dp(dz):
        return lax.rem(me_z + dz, nz) * ny + me_y

    def block(c, j):
        return main[c, j].reshape(rows, cb)

    def lanes_of(j):
        return pl.ds(pl.multiple_of(j * cb, 128), cb)

    barrier = pltpu.get_barrier_semaphore()

    def hello(where):
        pl.semaphore_signal(barrier, inc=1, device_id=where, device_id_type=pl.DeviceIdType.MESH)

    each(ni, lambda k: hello({"inner": inner_at(k)}))
    each(nx, lambda k: hello({"outer": outer_at(k)}))
    each(ndp, lambda k: hello({"dp": dp_at(k)}))
    for dz in range(1, nz):
        each(ni, lambda k, dz=dz: hello({"dp": far_dp(dz), "inner": inner_at(k)}))

    own = lanes_of(me_y)
    loads = [
        pltpu.make_async_copy(src, dst, loc.at[i])
        for i, (src, dst) in enumerate((
            (tokens.at[own], tokx),
            (tokens.at[pl.ds(mainw, tw)], ends_t.at[pl.ds(0, tw)]),
            (cot.at[pl.ds(mainw, tw)], ends_t.at[pl.ds(tw, tw)]),
            (cot.at[own], cotx),
            (router.at[pl.ds(pl.multiple_of(me_x * ni, ni), ni)], rrow),
            (w_in.at[0], wir),
            (w_out.at[0], wor),
        ))
    ]
    for load in loads:
        load.start()

    e, s = eid[...], sid[...]
    place_t[...] = (iota((rows, tcount), 0) == jnp.where(s >= 0, e * CAP + s, -1)).astype(BF)
    ends_t[2 * tw:] = jnp.zeros((128 - 2 * tw, tcount), BF)
    for load in loads[:3]:
        load.wait()
    s1a[:, :, :cb] = mm(place_t[...], tokx[...], 1, 1).astype(BF).reshape(nx, rx, cb)
    s1a[:, :, cb:] = mm(place_t[...], ends_t[...], 1, 1).astype(BF).reshape(nx, rx, 128)
    pl.semaphore_wait(barrier, (ni - 1) * nz + (nx - 1) + (ndp - 1))

    def a1(peer, slot):
        return send(s1a.at[peer], r1a.at[slot], a1_ss.at[peer], a1_rs.at[slot], {"outer": peer})

    def b1(peer, slot):
        return send(s1b.at[peer], r1b.at[slot], b1_ss.at[peer], b1_rs.at[slot], {"inner": peer})

    each(nx, lambda k: a1(outer_at(k), me_x).start())
    spot = jnp.where(s >= 0, (e & (ni - 1)) * ri + (e >> log2(ni)) * CAP + s, -1)
    place_b = (iota((rows, tcount), 0) == spot).astype(BF)
    loads[3].wait()
    s1b[...] = mm(place_b, cotx[...], 1, 1).astype(BF).reshape(ni, ri, cb)
    each(ni, lambda k: b1(inner_at(k), me_i).start())
    r1a[me_x] = s1a[me_x]
    r1b[me_i] = s1b[me_i]

    row, col = iota((rows, rows), 0), iota((rows, rows), 1)
    same_slot = (row & (CAP - 1)) == (col & (CAP - 1))
    row4, col4 = row >> log2(CAP), col >> log2(CAP)
    to_outer, to_inner = 0, 1
    swaps[to_outer] = (
        same_slot
        & ((row4 >> log2(ni)) == (col4 & (nx - 1)))
        & ((row4 & (ni - 1)) == (col4 >> log2(nx)))
    ).astype(BF)
    swaps[to_inner] = (
        same_slot
        & ((row4 >> log2(nx)) == (col4 & (ni - 1)))
        & ((row4 & (nx - 1)) == (col4 >> log2(ni)))
    ).astype(BF)

    def a2(q, peer, slot):
        src = (s2a if q == 0 else s2t).at[peer]
        dst = main.at[0, me_y, slot] if q == 0 else tail.at[slot]
        return send(src, dst, a2_ss.at[q, peer], a2_rs.at[q, slot], {"inner": peer})

    def b2(peer, slot):
        return send(s2b.at[peer], r2b.at[slot], b2_ss.at[peer], b2_rs.at[slot], {"outer": peer})

    each(nx, lambda k: a1(outer_at(k), outer_at(k)).wait())
    s2a[...] = mm(swaps[to_inner], r1a[:, :, :cb].reshape(rows, cb)).astype(BF).reshape(ni, ri, cb)
    each(ni, lambda k: a2(0, inner_at(k), me_i).start())
    s2t[...] = mm(swaps[to_inner], r1a[:, :, cb:].reshape(rows, 128)).astype(BF).reshape(ni, ri, 128)
    each(ni, lambda k: a2(1, inner_at(k), me_i).start())
    each(ni, lambda k: b1(inner_at(k), inner_at(k)).wait())
    s2b[...] = mm(swaps[to_outer], r1b[...].reshape(rows, cb)).astype(BF).reshape(nx, rx, cb)
    each(nx, lambda k: b2(outer_at(k), me_x).start())
    main[0, me_y, me_i] = s2a[me_i]
    tail[me_i] = s2t[me_i]
    r2b[me_x] = s2b[me_x]

    for load in loads[4:]:
        load.wait()
    rvec[:, :width] = jnp.broadcast_to(rrow[pl.ds(me_i, 1), :], (8, width))
    rvec[:, width:] = jnp.zeros((8, rvec.shape[1] - width), F32)
    wi2[:, :width] = wir[...]
    wi2[:, width:] = jnp.zeros((ff, wi2.shape[1] - width), BF)
    wo2[:, :width] = wor[...]
    wo2[:, width:] = jnp.zeros((ff, wo2.shape[1] - width), BF)

    def ag(c, way, t, j):
        ref = main.at[c, j]
        if t == steps - 1:
            ref = main.at[c, j, pl.ds(0 if way == 0 else ni // 2, ni // 2)]
        peer = right if way == 0 else left
        return send(ref, ref, ag_ss.at[c, way, t], ag_rs.at[c, way, t], {"dp": me_z * ny + peer})

    def ag_mine(c, way, t):
        return ag(c, way, t, y_at(-t if way == 0 else t))

    def ag_theirs(c, way, t):
        return ag(c, way, t, y_at(-t - 1 if way == 0 else t + 1))

    each(ni, lambda k: a2(0, inner_at(k), inner_at(k)).wait())
    for way in range(2):
        ag_mine(0, way, 0).start()
    each(nx, lambda k: b2(outer_at(k), outer_at(k)).wait())
    main[1, me_y] = mm(swaps[to_inner], r2b[...].reshape(rows, cb)).astype(BF).reshape(ni, ri, cb)
    for way in range(2):
        ag_mine(1, way, 0).start()
    each(ni, lambda k: a2(1, inner_at(k), inner_at(k)).wait())

    def reorder(d, carry):
        y, z = lax.rem(d, ny), lax.div(d, ny)
        at = pl.ds(pl.multiple_of(d * 128, 128), 256)
        part = pl.ds(pl.multiple_of(z * 128, 128), 128)
        pick = (iota((256, 128), 0) == iota((256, 128), 1) + 2 * d).astype(BF)
        wop[y, :, part] = mm(wo2[:, at], pick).astype(BF)
        wip[y, :, part] = mm(wi2[:, at], pick).astype(BF)
        return carry

    def tail_weights():
        shape = (ny * 16, wo2.shape[1])
        q, y = iota(shape, 0) & 15, iota(shape, 0) >> 4
        for first, ref in ((0, wo2), (2 * nz, wi2)):
            qq = q - first
            want = ((qq >> 1) * ny + y) * per + 128 + (qq & 1)
            pick = ((want == iota(shape, 1)) & (qq >= 0) & (qq < 2 * nz)).astype(BF)
            wtail[0 if first == 0 else 1] = mm(pick, ref[...], 1, 1).astype(BF)

    rpart[...] = stack3(rvec[...])
    rc = []
    for z in range(nz):
        d = z * ny + me_y
        piece = rvec[:, pl.ds(pl.multiple_of(d * 128, 128), 256)]
        mine = (me_z == z).astype(F32)
        rc.append(pltpu.roll(piece, lax.rem(256 - 2 * d, 256), 1)[0:1] * mine)
    drn[...] = jnp.zeros(drn.shape, F32)
    tail_rows = tail[...].reshape(rows, 128)
    pre = mm(tail_rows, wi2[:, mainw:], 1, 1)
    lg3 = mm(rpart[:, mainw:], tail_rows, 1, 1)

    def forward_block(j, pre, lg3):
        at = lanes_of(j)
        return (
            pre + mm(block(0, j), wi2[:, at], 1, 1),
            lg3 + mm(rpart[:, at], block(0, j), 1, 1),
        )

    pre, lg3 = forward_block(me_y, pre, lg3)
    wot[...] = mm(
        wo2[:, mainw:],
        ((iota((128, 128), 0) + tw == iota((128, 128), 1)) & (iota((128, 128), 0) < tw)).astype(BF),
    ).astype(BF)
    for t in range(1, steps + 1):
        for c in range(2 if t < steps else 1):
            for way in range(2):
                ag_theirs(c, way, t - 1).wait_recv()
                if t < steps:
                    ag_mine(c, way, t).start()
            if c == 0:
                pre, lg3 = forward_block(y_at(t), pre, lg3)
                if t < steps:
                    pre, lg3 = forward_block(y_at(-t), pre, lg3)
                    many = -(-ndp // (steps - 1))
                    lax.fori_loop((t - 1) * many, min(ndp, t * many), reorder, 0)
        if t == 1:
            tail_weights()

    gate_row = jax.nn.sigmoid(sum3(lg3))
    xs[...] = jnp.zeros(xs.shape, F32)
    xs[0:1, :] = gate_row
    gate_col = xs[...].T[:, 0:1]
    root, cubic = 0.7978845608028654, 0.044715
    tanh = jnp.tanh(root * (pre + cubic * (pre * pre * pre)))
    hid[...] = (0.5 * pre * (1.0 + tanh)).astype(BF)

    def rs_copy(way, t, c, z):
        src, dst = rs_s.at[way, t, c, z], rs_r.at[way, t, c, z]
        if t == 0:
            part = pl.ds(0 if way == 0 else half, half)
            src, dst = rs_s.at[0, 0, c, z, part], rs_r.at[way, 0, c, z, part]
        peer = right if way == 0 else left
        return send(src, dst, rm_ss.at[way, t, c, z], rm_rs.at[way, t, c, z], {"dp": me_z * ny + peer})

    def rt_copy(way, t):
        peer = right if way == 0 else left
        return send(rt_s.at[way, t], rt_r.at[way, t], rt_ss.at[way, t], rt_rs.at[way, t], {"dp": me_z * ny + peer})

    def partial(c, b):
        return mm(hid[...], wop[b]) if c == 0 else mm(gpr[...], wip[b])

    def cut(value, z):
        return value[:, z * 128:(z + 1) * 128]

    def rs_step(c, t):
        if t == 0:
            value = partial(c, y_at(steps))
            for z in range(nz):
                rs_s[0, 0, c, z] = cut(value, z).astype(BF)
                for way in range(2):
                    rs_copy(way, 0, c, z).start()
            return
        values = [partial(c, y_at(steps - t)), partial(c, y_at(t - steps))]
        for z in range(nz):
            for way in range(2):
                value = cut(values[way], z)
                rs_copy(way, t - 1, c, z).wait_recv()
                if t == 1:
                    part = slice(0, half) if way == 0 else slice(half, rows)
                    rest = slice(half, rows) if way == 0 else slice(0, half)
                    rs_s[way, t, c, z, part] = (value[part] + rs_r[way, 0, c, z, part].astype(F32)).astype(BF)
                    rs_s[way, t, c, z, rest] = value[rest].astype(BF)
                else:
                    rs_s[way, t, c, z] = (value + rs_r[way, t - 1, c, z].astype(F32)).astype(BF)
                rs_copy(way, t, c, z).start()

    def rt_step(t):
        if t == 0:
            tails_t[...] = (mm(wtail[0], hid[...], 1, 1) + mm(wtail[1], gpr[...], 1, 1)).reshape(ny, 16, rows)
            rt_s[0, 0] = tails_t[y_at(steps)].astype(BF)
            rt_copy(0, 0).start()
            return
        for way in range(2):
            ends = tails_t[y_at(steps - t if way == 0 else t - steps)]
            if way == 0 or t > 1:
                rt_copy(way, t - 1).wait_recv()
                ends = ends + rt_r[way, t - 1].astype(F32)
            rt_s[way, t] = ends.astype(BF)
            rt_copy(way, t).start()

    def rs_last(c, value, z):
        for way in range(2):
            rs_copy(way, steps - 1, c, z).wait_recv()
        return cut(value, z) + rs_r[0, steps - 1, c, z].astype(F32) + rs_r[1, steps - 1, c, z].astype(F32)

    def s_copy(k, slot):
        return send(sbuf.at[me_d], sbuf.at[slot], s_ss.at[dp_at(k)], s_rs.at[slot], {"dp": dp_at(k)})

    def d1_copy(k, slot):
        return send(dr1.at[me_i], dr1.at[slot], d1_ss.at[inner_at(k)], d1_rs.at[slot], {"inner": inner_at(k)})

    def d2_copy(k, slot):
        return send(dro.at[me_x], dro.at[slot], d2_ss.at[outer_at(k)], d2_rs.at[slot], {"outer": outer_at(k)})

    def p3(c, peer, slot):
        s3, r3 = ((s3m, r3m), (s3t, r3t))[c]
        return send(s3.at[peer], r3.at[slot], p3_ss.at[c, peer], p3_rs.at[c, slot], {"outer": peer})

    def p4(c, z, peer, slot_z, slot_i):
        s4, r4 = ((s4m, r4m), (s4t, r4t))[c]
        return send(
            s4.at[z, peer], r4.at[slot_z, slot_i], p4_ss.at[c, z, peer], p4_rs.at[c, slot_z, slot_i],
            {"dp": z * ny + me_y, "inner": peer},
        )

    def p3_start(c):
        each(nx, lambda k: p3(c, outer_at(k), me_x).start())

    def p3_wait(c):
        each(nx, lambda k: p3(c, outer_at(k), outer_at(k)).wait())

    def p4_all(act):
        for dz in range(nz):
            z = lax.rem(me_z + dz, nz)
            each(ni, lambda k, z=z: act(z, inner_at(k)), 1 if dz == 0 else 0)

    def p4_start(c):
        p4_all(lambda z, peer: p4(c, z, peer, me_z, me_i).start())

    def p4_wait(c):
        p4_all(lambda z, peer: p4(c, z, peer, z, peer).wait())

    rs_step(0, 0)
    for way in range(2):
        ag_theirs(1, way, steps - 1).wait_recv()
    slope = 0.5 * (1.0 + tanh) + 0.5 * pre * (1.0 - tanh * tanh) * (
        root * (1.0 + (3.0 * cubic) * (pre * pre))
    )
    tails_scaled = (gate_col * tail_rows.astype(F32)).astype(BF)
    grad = mm(tails_scaled, wot[...], 1, 1)

    def scale_block(j, total):
        scaled = (gate_col * block(1, j).astype(F32)).astype(BF)
        scl[j] = scaled
        return total + mm(scaled, wo2[:, lanes_of(j)], 1, 1)

    grad = lax.fori_loop(0, ny, scale_block, grad)
    gpr[...] = (slope * grad).astype(BF)
    rs_step(1, 0)
    rt_step(0)
    rs_step(0, 1)
    product = hid[...].astype(F32) * grad
    dots = lax.dot_general(
        jnp.ones((8, ff), F32), product, (((1,), (1,)), ((), ())),
        precision=lax.Precision.HIGHEST, preferred_element_type=F32,
    )
    sbuf[me_d] = dots[0:1]
    each(ndp, lambda k: s_copy(k, me_d).start())
    def weight_grads(j, carry):
        at = lanes_of(j)
        dwi[:, at] = mm(gpr[...], block(0, j), 0, 0).astype(BF)
        dwo[:, at] = mm(hid[...], scl[j], 0, 0).astype(BF)
        return carry

    def gate_grads():
        each(ndp, lambda k: s_copy(k, dp_at(k)).wait())
        total = sbuf[0]
        for k in range(1, ndp):
            total = total + sbuf[k]
        lg_row = total * (1.0 - gate_row)
        xs[1:2, :] = lg_row
        lgs = stack3(lg_row)
        for j in range(ny):
            drn[0:1, j * cb:(j + 1) * cb] = sum3(mm(lgs, block(0, j)))
        drn[0:1, mainw:] = sum3(mm(lgs, tail_rows))
        piece = drn[:, pl.ds(pl.multiple_of(me_d * 128, 128), 256)]
        dr1[me_i] = pltpu.roll(piece, lax.rem(256 - 2 * me_d, 256), 1)[0:1]
        each(ni, lambda k: d1_copy(k, me_i).start())

    done = 0
    for t in range(1, steps):
        rt_step(t)
        rs_step(1, t)
        for later in range(2 if t < steps - 1 else 0):
            if later:
                rs_step(0, t + 1)
            if later and t == steps - 2:
                gate_grads()
            else:
                upto = min(ny, done + 3)
                lax.fori_loop(done, upto, weight_grads, 0)
                done = upto
    lax.fori_loop(done, ny, weight_grads, 0)
    if steps < 3:
        gate_grads()

    lg_row = xs[1:2, :]
    ends = tails_t[me_y]
    for way in range(2):
        rt_copy(way, steps - 1).wait_recv()
        ends = ends + rt_r[way, steps - 1].astype(F32)
    xs[8:24, :] = ends
    for q in range(2 * nz):
        xs[8 + q:9 + q, :] = xs[8 + q:9 + q, :] * gate_row
        z, k = q // 2, q % 2
        at = 8 + 2 * nz + q
        xs[at:at + 1, :] = xs[at:at + 1, :] + lg_row * rc[z][:, 128 + k:129 + k]
    turned = xs[...].T
    lg_col = turned[:, 1:2]
    ends = turned.astype(BF).reshape(ni, ri, 128)
    value = partial(0, me_y)
    for z in range(nz):
        s4m[z, :, :, 128:] = ends
        s4m[z, :, :, :128] = (gate_col * rs_last(0, value, z)).astype(BF).reshape(ni, ri, 128)
    p4_start(0)
    r4m[me_z, me_i] = s4m[me_z, me_i]
    value = partial(1, me_y)
    for z in range(nz):
        piece = rs_last(1, value, z) + lg_col * rc[z][:, :128]
        s4t[z] = piece.astype(BF).reshape(ni, ri, 128)
    p4_start(1)
    r4t[me_z, me_i] = s4t[me_z, me_i]
    dwi[:, mainw:width] = mm(gpr[...], tail_rows, 0, 0)[:, :tw].astype(BF)
    dwo[:, mainw:width] = mm(hid[...], tails_scaled, 0, 0)[:, tw:2 * tw].astype(BF)
    stores = [
        pltpu.make_async_copy(dwi, d_win.at[0], loc.at[7]),
        pltpu.make_async_copy(dwo, d_wout.at[0], loc.at[8]),
    ]
    for store in stores:
        store.start()

    def onward(c):
        r4, s3, r3 = ((r4m, s3m, r3m), (r4t, s3t, r3t))[c]
        p4_wait(c)
        value = r4[0].astype(F32)
        for z in range(1, nz):
            value = value + r4[z].astype(F32)
        value = value.astype(BF).reshape(rows, r4.shape[-1])
        s3[...] = mm(swaps[to_outer], value).astype(BF).reshape(s3.shape)
        p3_start(c)
        r3[me_x] = s3[me_x]

    onward(0)
    each(ni, lambda k: d1_copy(k, inner_at(k)).wait())
    for k in range(ni):
        dro[me_x, k:k + 1] = dr1[k]
    each(nx, lambda k: d2_copy(k, me_x).start())
    onward(1)

    def arrived(r3):
        return mm(r3[...].reshape(rows, r3.shape[-1]), place_t[...], 0, 0)

    p3_wait(0)
    result = arrived(r3m)
    mixed[:128] = result[:128].astype(BF)
    ends = result[136:138]
    more = result[136 + 2 * nz:138 + 2 * nz]
    for z in range(1, nz):
        at = 136 + 2 * z
        ends = jnp.where(me_z == z, result[at:at + 2], ends)
        more = jnp.where(me_z == z, result[at + 2 * nz:at + 2 * nz + 2], more)
    mixed[128:per] = ends.astype(BF)
    d_tok[128:per] = more.astype(BF)
    each(nx, lambda k: d2_copy(k, outer_at(k)).wait())
    drt[...] = dro[...].reshape(experts, 256)
    d_router[...] = drt[:, :per]

    for c in range(2):
        for way in range(2):
            for t in range(steps):
                ag_mine(c, way, t).wait_send()
                for z in range(nz):
                    rs_copy(way, t, c, z).wait_send()
    for way in range(2):
        for t in range(steps):
            if way == 0 or t > 0:
                rt_copy(way, t).wait_send()
    p3_wait(1)
    d_tok[:128] = arrived(r3t).astype(BF)
    for store in stores:
        store.wait()


def store(*refs):
    ins, outs, held, sems = refs[:5], refs[5:10], refs[10:15], refs[15]
    loads = [pltpu.make_async_copy(ins[i], held[i], sems.at[0, i]) for i in range(5)]
    stores = [pltpu.make_async_copy(held[i], outs[i], sems.at[1, i]) for i in range(5)]
    for copy in loads:
        copy.start()
    for load, copy in zip(loads, stores):
        load.wait()
        copy.start()
    for copy in stores:
        copy.wait()


def on_device(nz, tokens, cotangent, expert_id, slot_id, router, w_in, w_out):
    ndp, nx, ni = lax.axis_size("dp"), lax.axis_size("outer"), lax.axis_size("inner")
    ny = ndp // nz
    steps = ny // 2
    tcount, width = tokens.shape
    experts = nx * ni
    rows = experts * CAP
    ri, rx = nx * CAP, ni * CAP
    cb = nz * 128
    padded = (ndp + 1) * 128
    per = width // ndp
    ff = w_in.shape[2]
    dma = pltpu.SemaphoreType.DMA
    vm = pltpu.VMEM
    scratch = [
        vm((cb, tcount), BF), vm((cb, tcount), BF), vm((128, tcount), BF), vm((ni, width), F32),
        vm((ff, width), BF), vm((ff, width), BF), vm((ff, width), BF), vm((ff, width), BF),
        vm((nx, rx, cb + 128), BF), vm((ni, ri, cb), BF), vm((nx, rx, cb + 128), BF), vm((ni, ri, cb), BF),
        vm((ni, ri, cb), BF), vm((ni, ri, 128), BF), vm((nx, rx, cb), BF), vm((nx, rx, cb), BF),
        vm((2, ny, ni, ri, cb), BF), vm((ni, ri, 128), BF), vm((ny, rows, cb), BF), vm((2, rows, rows), BF),
        vm((ff, padded), BF), vm((ff, padded), BF), vm((ff, 128), BF), vm((ny, ff, cb), BF), vm((ny, ff, cb), BF),
        vm((2, ny * 16, ff), BF), vm((8, padded), F32), vm((16, padded), BF), vm((rows, tcount), BF),
        vm((rows, ff), BF), vm((rows, ff), BF), vm((2, steps, 2, nz, rows, 128), BF), vm((2, steps, 2, nz, rows, 128), BF),
        vm((2, steps, 16, rows), BF), vm((2, steps, 16, rows), BF), vm((ny, 16, rows), F32), vm((128, rows), F32),
        vm((ndp, 1, rows), F32), vm((8, padded), F32), vm((ni, 1, 256), F32), vm((nx, ni, 256), F32), vm((experts, 256), F32),
        vm((nx, rx, 256), BF), vm((nx, rx, 256), BF), vm((nx, rx, 128), BF), vm((nx, rx, 128), BF),
        vm((nz, ni, ri, 256), BF), vm((nz, ni, ri, 256), BF), vm((nz, ni, ri, 128), BF), vm((nz, ni, ri, 128), BF),
        dma((9,)), dma((nx,)), dma((nx,)), dma((2, ni)), dma((2, ni)), dma((ni,)), dma((ni,)), dma((nx,)), dma((nx,)),
        dma((2, 2, steps)), dma((2, 2, steps)), dma((ndp,)), dma((ndp,)),
        dma((2, steps, 2, nz)), dma((2, steps, 2, nz)), dma((2, steps)), dma((2, steps)),
        dma((2, nx)), dma((2, nx)), dma((2, nz, ni)), dma((2, nz, ni)), dma((ni,)), dma((ni,)), dma((nx,)), dma((nx,)),
    ]
    shape = jax.ShapeDtypeStruct
    outs = pl.pallas_call(
        functools.partial(kernel, nz),
        out_shape=(
            shape((per, tcount), BF), shape((per, tcount), BF),
            shape(w_out.shape, BF), shape(w_out.shape, BF), shape((experts, per), F32),
        ),
        in_specs=[pl.BlockSpec(memory_space=pltpu.VMEM)] * 2 + [pl.BlockSpec(memory_space=pl.ANY)] * 5,
        out_specs=tuple(
            pl.BlockSpec(memory_space=space)
            for space in (pltpu.VMEM, pltpu.VMEM, pl.ANY, pl.ANY, pltpu.VMEM)
        ),
        scratch_shapes=scratch,
        compiler_params=pltpu.CompilerParams(
            collective_id=0, has_side_effects=True, vmem_limit_bytes=VMEM_LIMIT
        ),
    )(
        expert_id.reshape(1, tcount), slot_id.reshape(1, tcount), tokens.T, cotangent.T, router.T,
        jnp.swapaxes(w_in, 1, 2), w_out,
    )
    mixed, d_tok, d_win, d_wout, d_router = pl.pallas_call(
        store,
        out_shape=tuple(shape(out.shape, out.dtype) for out in outs),
        in_specs=[pl.BlockSpec(memory_space=pl.ANY)] * 5,
        out_specs=tuple([pl.BlockSpec(memory_space=pl.ANY)] * 5),
        scratch_shapes=[vm(out.shape, out.dtype) for out in outs] + [dma((2, 5))],
        compiler_params=pltpu.CompilerParams(vmem_limit_bytes=VMEM_LIMIT),
    )(*outs)
    return mixed.T, d_tok.T, jnp.swapaxes(d_win, 1, 2), d_wout, d_router.T


def build(mesh, nz):
    return jax.shard_map(
        functools.partial(on_device, nz),
        mesh=mesh,
        in_specs=(
            P(("outer", "inner"), None),
            P(("outer", "inner"), None),
            P(("outer", "inner")),
            P(("outer", "inner")),
            P(),
            P(("outer", "inner"), None, "dp"),
            P(("outer", "inner"), "dp", None),
        ),
        out_specs=(
            P(("outer", "inner"), "dp"),
            P(("outer", "inner"), "dp"),
            P(("outer", "inner"), None, "dp"),
            P(("outer", "inner"), "dp", None),
            P("dp", None),
        ),
        check_vma=False,
    )


def solution(mesh):
    return build(mesh, NZ)
```
